32 devices in a mesh: rep: 2 (over core), fsdp: 16 (over z, y, x).
Axes of the slice: x: 2, y: 2, z: 4, core: 2. Of those that a mesh axis runs over, the one named last changes fastest.
Arguments:
- hidden: bfloat16 [24576, 768], P(('rep', 'fsdp')), may hold values from -6 to 6
- qry_len: int32 [64], P(('rep', 'fsdp')), may hold values from 103 to 128, as said below
- psg_len: int32 [32], P(('rep', 'fsdp')), may hold values from 410 to 512, as said below
- qry_grad: float32 [64, 768], P(('rep', 'fsdp')), may hold values from -192 to 192
- psg_grad: float32 [32, 768], P(('rep', 'fsdp')), may hold values from -192 to 192
- w_qkv: bfloat16 [2, 768, 2304], P(None, 'fsdp'), may hold values from -0.21875 to 0.21875
- w_o: bfloat16 [2, 768, 768], P(None, 'fsdp'), may hold values from -0.625 to 0.625
- w_in: bfloat16 [2, 768, 3072], P(None, 'fsdp'), may hold values from -0.21875 to 0.21875
- w_out: bfloat16 [2, 3072, 768], P(None, 'fsdp'), may hold values from -0.109375 to 0.109375
- biases: bfloat16 [2, 6, 768], P(None, None, 'fsdp'), may hold values from -1.75 to 1.75
- gains: bfloat16 [2, 2, 768], P(None, None, 'fsdp'), may hold values from 0.25 to 1.75
- in_bias: bfloat16 [2, 3072], P(None, 'fsdp'), may hold values from -1.75 to 1.75
Outputs:
- mixed: bfloat16 [24576, 768], P(('rep', 'fsdp'))
- grad_hidden: bfloat16 [24576, 768], P(('rep', 'fsdp'))
- grad_qkv: float32 [2, 768, 2304], P(None, 'fsdp')
- grad_o: float32 [2, 768, 768], P(None, 'fsdp')
- grad_in: float32 [2, 768, 3072], P(None, 'fsdp')
- grad_out: float32 [2, 3072, 768], P(None, 'fsdp')
- grad_biases: float32 [2, 6, 768], P(None, None, 'fsdp')
- grad_gains: float32 [2, 2, 768], P(None, None, 'fsdp')
- grad_in_bias: float32 [2, 3072], P(None, 'fsdp')
The draws below stay inside these ranges and needn't reach their ends.
Inputs may be any that keep to these rules, and one draw needn't show every extreme that they name: `qry_len`: each query has 103 to 128 live slots; some query has all 128. `psg_len`: each passage has 410 to 512 live slots; some passage has all 512.
All inputs are finite; a program needn't handle non-finite values.
Results may differ from the reference program's by a relative error of at most 0.017.
Values may be sent and summed in bfloat16 or wider, within the bound.
A program may use at most 320 MiB of HBM per device.

```python
import jax
import jax.numpy as jnp
from jax import lax

D = 768
H = 12
HD = 64
FF = 3072
LAYERS = 2
SHORT = 128
LONG = 512
PSG_DEV = 1
QRY_DEV = 2
TOK_DEV = 768
QUERIES = 64
PASSAGES = 32
TOKENS = 24576
DEVICES = 32


def draw_lengths(key, how_many, longest):
    lengths_drawn = jax.random.randint(key, (how_many,), longest - longest // 5, longest + 1)
    chosen = jax.random.randint(jax.random.fold_in(key, 7), (), 0, how_many)
    return lengths_drawn.at[chosen].set(longest).astype(jnp.int32)


def draw_qry_len(key, part):
    key = jax.random.fold_in(key, 1)
    return draw_lengths(key, QUERIES, SHORT)


def draw_psg_len(key, part):
    key = jax.random.fold_in(key, 2)
    return draw_lengths(key, PASSAGES, LONG)


def levels(own_key, dims, split, smallest, largest):
    factor_of = 1.0
    for axis_at, parts in split:
        steps = jax.random.uniform(jax.random.fold_in(jax.random.fold_in(own_key, 6), axis_at), (parts,), jnp.float32, smallest / len(split), largest / len(split))
        factor_of = factor_of * jnp.repeat(jnp.exp(steps), dims[axis_at] // parts).reshape((-1,) + (1,) * (len(dims) - 1 - axis_at))
    return factor_of


def scatter_about(rng, extent, scale, reach, pieces=(), held_as=jnp.bfloat16):
    level = levels(rng, extent, pieces, -0.22, 0.18) if pieces else 1.0
    entries = jax.random.normal(rng, extent, jnp.float32) * scale * level
    return jnp.minimum(jnp.maximum(entries, -reach), reach).astype(held_as)


def setup_inputs(seed: int = 0) -> dict:
    key_of = jax.random.split(jax.random.key(seed), 13)
    hidden = scatter_about(key_of[0], (TOKENS, D), 1.0, 6.0, ((0, 32),))
    qry_len = draw_qry_len(jax.random.fold_in(key_of[12], 71), 0)
    psg_len = draw_psg_len(jax.random.fold_in(key_of[12], 71), 0)
    qry_grad = scatter_about(key_of[3], (QUERIES, D), 32.0, 192.0, ((0, 32),), jnp.float32)
    psg_grad = scatter_about(key_of[4], (PASSAGES, D), 32.0, 192.0, ((0, 32),), jnp.float32)
    w_qkv = scatter_about(key_of[5], (LAYERS, D, 3 * D), D ** -0.5, 0.21875, ((1, 16),))
    w_o = scatter_about(key_of[6], (LAYERS, D, D), (D // 8) ** -0.5, 0.625, ((1, 16),))
    w_in = scatter_about(key_of[7], (LAYERS, D, FF), D ** -0.5, 0.21875, ((1, 16),))
    w_out = scatter_about(key_of[8], (LAYERS, FF, D), FF ** -0.5, 0.109375, ((1, 16),))
    biases = scatter_about(key_of[9], (LAYERS, 6, D), 0.3, 1.75, ((2, 16),))
    gains = jnp.clip(1.0 + 0.15 * jax.random.normal(key_of[10], (LAYERS, 2, D), jnp.float32), 0.25, 1.75).astype(jnp.bfloat16)
    in_bias = scatter_about(key_of[11], (LAYERS, FF), 0.3, 1.75, ((1, 16),))
    return {"hidden": hidden, "qry_len": qry_len, "psg_len": psg_len, "qry_grad": qry_grad, "psg_grad": psg_grad, "w_qkv": w_qkv, "w_o": w_o, "w_in": w_in, "w_out": w_out, "biases": biases, "gains": gains, "in_bias": in_bias}


PRECISE = lax.Precision.HIGHEST
NORM_EPS = 1e-12
MASKED = -1e+30

@jax.custom_vjp
def low(v):
    return lax.optimization_barrier(v.astype(jnp.bfloat16)).astype(jnp.float32)

@jax.custom_vjp
def low_back(v):
    return v

def low_keep(v):
    return (low(v), None)

def low_pass(kept, grad):
    return (grad,)

def back_keep(v):
    return (v, None)

def back_low(kept, grad):
    return (low(grad),)
low.defvjp(low_keep, low_pass)
low_back.defvjp(back_keep, back_low)

def norm_rows(resid, gain, shift):
    average = lax.optimization_barrier(jnp.mean(resid, axis=-1, keepdims=True))
    centered = resid - average
    spread = lax.optimization_barrier(jnp.mean(centered * centered, axis=-1, keepdims=True))
    return centered * lax.rsqrt(spread + NORM_EPS) * gain + shift

def attend_kind(packed, lengths):
    query_rows = packed[:, :, 0]
    key_rows = packed[:, :, 1]
    value_rows = packed[:, :, 2]
    score_scale = query_rows.shape[-1] ** (-0.5)
    scores = low_back(jnp.einsum('bqhd,bkhd->bhqk', query_rows, key_rows, precision=PRECISE) * score_scale)
    visible = jnp.arange(key_rows.shape[1])[None, :] < lengths[:, None]
    scores = jnp.where(visible[:, None, None, :], scores, MASKED)
    highest = lax.optimization_barrier(jnp.max(scores, axis=-1, keepdims=True))
    exponentials = jnp.exp(scores - highest)
    probabilities = exponentials / lax.optimization_barrier(jnp.sum(exponentials, axis=-1, keepdims=True))
    return jnp.einsum('bhqk,bkhd->bqhd', low(probabilities), value_rows, precision=PRECISE)

def attend_block(block):
    packed_rows, short_len, long_len = block
    cut = QRY_DEV * SHORT
    short_pack = packed_rows[:cut].reshape(QRY_DEV, SHORT, 3, H, HD)
    long_pack = packed_rows[cut:].reshape(PSG_DEV, LONG, 3, H, HD)
    short_context = attend_kind(short_pack, short_len).reshape(QRY_DEV * SHORT, D)
    long_context = attend_kind(long_pack, long_len).reshape(PSG_DEV * LONG, D)
    return jnp.concatenate([short_context, long_context], axis=0)

def layer_forward(inputs, w_qkv, w_o, w_in, w_out, bias_rows, gain_rows, in_bias, qry_len, psg_len):
    inputs_low = low(inputs)
    qkv_bias = jnp.concatenate([bias_rows[0], jnp.zeros_like(bias_rows[0]), bias_rows[1]])
    packed = low(low_back(jnp.dot(inputs_low, w_qkv, precision=PRECISE) + qkv_bias))
    blocks = packed.reshape(DEVICES, TOK_DEV, 3, H, HD)
    context = lax.map(jax.checkpoint(attend_block), (blocks, qry_len.reshape(DEVICES, QRY_DEV), psg_len.reshape(DEVICES, PSG_DEV)))
    context_low = low(low_back(context.reshape(TOKENS, D)))
    attended = low_back(jnp.dot(context_low, w_o, precision=PRECISE)) + bias_rows[2]
    first_norm = norm_rows(inputs + attended, gain_rows[0], bias_rows[3])
    upward = low_back(jnp.dot(low(first_norm), w_in, precision=PRECISE)) + in_bias
    active = low(jax.nn.gelu(upward, approximate=False))
    downward = low_back(jnp.dot(active, w_out, precision=PRECISE)) + bias_rows[4]
    return norm_rows(first_norm + downward, gain_rows[1], bias_rows[5])

def network(hidden_float, w_qkv, w_o, w_in, w_out, biases, gains, in_bias, qry_len, psg_len):
    state = hidden_float
    for which_layer in range(LAYERS):
        state = layer_forward(state, w_qkv[which_layer], w_o[which_layer], w_in[which_layer], w_out[which_layer], biases[which_layer], gains[which_layer], in_bias[which_layer], qry_len, psg_len)
    rows = state.reshape(DEVICES, TOK_DEV, D)
    cut = QRY_DEV * SHORT
    short_rows = rows[:, :cut].reshape(QUERIES, SHORT, D)
    long_rows = rows[:, cut:].reshape(PASSAGES, LONG, D)
    short_mask = (jnp.arange(SHORT)[None, :] < qry_len[:, None]).astype(jnp.float32)
    long_mask = (jnp.arange(LONG)[None, :] < psg_len[:, None]).astype(jnp.float32)
    pooled_short = lax.optimization_barrier(jnp.sum(short_rows * short_mask[:, :, None], axis=1)) / qry_len.astype(jnp.float32)[:, None]
    pooled_long = lax.optimization_barrier(jnp.sum(long_rows * long_mask[:, :, None], axis=1)) / psg_len.astype(jnp.float32)[:, None]
    return ((pooled_short, pooled_long), state)

def reference(hidden, qry_len, psg_len, qry_grad, psg_grad, w_qkv, w_o, w_in, w_out, biases, gains, in_bias):

    def forward_floats(hidden_float, qkv_float, o_float, in_float, out_float, biases_float, gains_float, in_bias_float):
        return network(hidden_float, qkv_float, o_float, in_float, out_float, biases_float, gains_float, in_bias_float, qry_len, psg_len)
    pooled, pull_back, final = jax.vjp(forward_floats, hidden.astype(jnp.float32), w_qkv.astype(jnp.float32), w_o.astype(jnp.float32), w_in.astype(jnp.float32), w_out.astype(jnp.float32), biases.astype(jnp.float32), gains.astype(jnp.float32), in_bias.astype(jnp.float32), has_aux=True)
    grads = pull_back((qry_grad, psg_grad))
    return (final.astype(jnp.bfloat16), grads[0].astype(jnp.bfloat16), grads[1], grads[2], grads[3], grads[4], grads[5], grads[6], grads[7])
```

```python
import functools
import jax
import jax.numpy as jnp
from jax import lax
from jax.experimental import pallas as pl
from jax.experimental.pallas import tpu as pltpu

from jax.sharding import PartitionSpec as P

MESH = pl.DeviceIdType.MESH
D = 768
H = 12
HD = 64
SHORT = 128
LONG = 512
BLK = 16
PAIR = 2 * BLK
LAG = 2
DEPTH = 4
ROUTES = (
    ("xzy", 0, 128),
    ("yzx", 128, 128),
    ("zxy", 256, 256),
    ("zyx", 512, 256),
)


def place():
    core = lax.axis_index("rep")
    spot = lax.axis_index("fsdp")
    return core, lax.rem(spot, 2), lax.rem(spot // 2, 2), spot // 4


def partner(axis, step=1):
    core, x, y, z = place()
    if axis == "c":
        core = 1 - core
    elif axis == "x":
        x = 1 - x
    elif axis == "y":
        y = 1 - y
    else:
        z = lax.rem(z + step, 4)
    return (core, z * 4 + y * 2 + x)


def greet():
    barrier = pltpu.get_barrier_semaphore()
    others = [("c", 1), ("x", 1), ("y", 1), ("z", 1), ("z", 2), ("z", 3)]
    for axis, step in others:
        pl.semaphore_signal(
            barrier, inc=1, device_id=partner(axis, step), device_id_type=MESH
        )
    pl.semaphore_wait(barrier, len(others))


def steps_of(axis):
    return (1, 2, 3) if axis == "z" else (1,)


SLOTS = {}
for _route, (_order, _a, _b) in enumerate(ROUTES):
    for _stage in range(3):
        for _step in steps_of(_order[_stage]):
            SLOTS[(_route, _stage, _step)] = len(SLOTS)
CORE_SLOT = len(SLOTS)
FINAL_SLOT = CORE_SLOT + 1
SLOT_COUNT = CORE_SLOT + 2


def when_in(chunk, count, work):
    if isinstance(chunk, int):
        if 0 <= chunk < count:
            work()
    else:
        pl.when(jnp.logical_and(chunk >= 0, chunk < count))(work)


def gather_rows(chunk, core, count):
    spot = lax.rem(chunk + count - 1, count)
    return pl.ds(pl.multiple_of(spot * PAIR + core * BLK, BLK), BLK)


def scatter_rows(chunk, core, count):
    spot = lax.rem(2 * count - 2 - chunk, count)
    return pl.ds(pl.multiple_of(spot * PAIR + core * BLK, BLK), BLK)


class Gather:
    def __init__(self, own, whole, send, recv, local, count):
        self.own, self.whole, self.send, self.recv = own, whole, send, recv
        self.local = local
        self.count = count
        self.rounds = count + 4 * LAG

    def copies(self, chunk, stage):
        core, x, y, z = place()
        slot = lax.rem(chunk, DEPTH)
        if stage == 3:
            rows = gather_rows(chunk, core, self.count)
            part = self.whole.at[:, :, :, rows, :]
            return [
                pltpu.make_async_remote_copy(
                    src_ref=part,
                    dst_ref=part,
                    send_sem=self.send.at[CORE_SLOT, slot],
                    recv_sem=self.recv.at[CORE_SLOT, slot],
                    device_id=partner("c"),
                    device_id_type=MESH,
                )
            ]
        rows = gather_rows(chunk, core, self.count)
        found = []
        for route, (order, first, width) in enumerate(ROUTES):
            axis = order[stage]
            done = order[:stage]
            columns = pl.ds(first, width)
            spans = [
                pl.ds(0, size) if name in done else pl.ds(at, 1)
                for name, at, size in (("z", z, 4), ("y", y, 2), ("x", x, 2))
            ]
            part = self.whole.at[spans[0], spans[1], spans[2], rows, columns]
            if stage == 0:
                source = self.own.at[rows, columns]
                part = self.whole.at[z, y, x, rows, columns]
            else:
                source = part
            for step in steps_of(axis):
                index = SLOTS[(route, stage, step)]
                found.append(
                    pltpu.make_async_remote_copy(
                        src_ref=source,
                        dst_ref=part,
                        send_sem=self.send.at[index, slot],
                        recv_sem=self.recv.at[index, slot],
                        device_id=partner(axis, step),
                        device_id_type=MESH,
                    )
                )
        return found

    def keep(self, chunk):
        core, x, y, z = place()
        rows = gather_rows(chunk, core, self.count)
        return pltpu.make_async_copy(
            self.own.at[rows, :],
            self.whole.at[z, y, x, rows, :],
            self.local.at[lax.rem(chunk, DEPTH)],
        )

    def round(self, number):
        for stage in range(4):
            chunk = number - LAG * stage - LAG

            def finish(chunk=chunk, stage=stage):
                for copy in self.copies(chunk, stage):
                    copy.wait()
                if stage == 0:
                    self.keep(chunk).wait()

            when_in(chunk, self.count, finish)
        for stage in range(4):
            chunk = number - LAG * stage

            def begin(chunk=chunk, stage=stage):
                for copy in self.copies(chunk, stage):
                    copy.start()
                if stage == 0:
                    self.keep(chunk).start()

            when_in(chunk, self.count, begin)


def gather_kernel(count, own, whole, send, recv, local):
    greet()
    rounds = Gather(own, whole, send, recv, local, count)

    def body(number, carry):
        rounds.round(number)
        return carry

    lax.fori_loop(0, rounds.rounds, body, 0)


def gather(own):
    rows = own.shape[0]
    return pl.pallas_call(
        functools.partial(gather_kernel, rows // PAIR),
        out_shape=jax.ShapeDtypeStruct((4, 2, 2, rows, D), own.dtype),
        in_specs=[pl.BlockSpec(memory_space=pl.ANY)],
        out_specs=pl.BlockSpec(memory_space=pl.ANY),
        scratch_shapes=[
            pltpu.SemaphoreType.DMA((SLOT_COUNT, DEPTH)),
            pltpu.SemaphoreType.DMA((SLOT_COUNT, DEPTH)),
            pltpu.SemaphoreType.DMA((DEPTH,)),
        ],
        compiler_params=pltpu.CompilerParams(
            collective_id=0, has_side_effects=True, vmem_limit_bytes=48 * 2**20
        ),
        name="gather_weights",
    )(own)


class Scatter:
    def __init__(self, partial, total, work, send, recv, local, count):
        self.partial, self.total, self.work = partial, total, work
        self.send, self.recv, self.local = send, recv, local
        self.count = count
        self.rounds = count + 5 * LAG

    def rows(self, chunk, core):
        return scatter_rows(chunk, core, self.count)

    def load(self, chunk):
        core = place()[0]
        slot = lax.rem(chunk, DEPTH)
        return pltpu.make_async_copy(
            self.partial.at[:, :, :, self.rows(chunk, core), :],
            self.work["mine"].at[slot],
            self.local.at[0, slot],
        )

    def store(self, chunk):
        core = place()[0]
        slot = lax.rem(chunk, DEPTH)
        return pltpu.make_async_copy(
            self.work["final"].at[slot],
            self.total.at[self.rows(chunk, core), :],
            self.local.at[1, slot],
        )

    def remote(self, src, dst, index, slot, device):
        return pltpu.make_async_remote_copy(
            src_ref=src,
            dst_ref=dst,
            send_sem=self.send.at[index, slot],
            recv_sem=self.recv.at[index, slot],
            device_id=device,
            device_id_type=MESH,
        )

    def copies(self, chunk, stage):
        core, x, y, z = place()
        slot = lax.rem(chunk, DEPTH)
        if stage == 0:
            return [
                self.remote(
                    self.partial.at[:, :, :, self.rows(chunk, 1 - core), :],
                    self.work["theirs"].at[slot],
                    CORE_SLOT,
                    slot,
                    partner("c"),
                )
            ]
        if stage == 4:
            return [
                self.remote(
                    self.work["final"].at[slot],
                    self.total.at[self.rows(chunk, core), :],
                    FINAL_SLOT,
                    slot,
                    partner("c"),
                )
            ]
        found = []
        at = {"x": x, "y": y, "z": z}
        for route, (gather_order, first, width) in enumerate(ROUTES):
            order = gather_order[::-1]
            axis = order[stage - 1]
            left = [name for name in "zyx" if name not in order[: stage - 1]]
            if stage == 1:
                held = self.work["pair"].at[slot]
                columns = pl.ds(first, width)
            else:
                held = self.work["held", route, stage - 1].at[slot]
                columns = slice(None)
            landing = self.work["land", route, stage].at[slot]
            for step in steps_of(axis):
                if axis == "z":
                    to = lax.rem(z + step, 4)
                else:
                    to = 1 - at[axis]
                index = tuple(to if name == axis else slice(None) for name in left)
                found.append(
                    self.remote(
                        held.at[index + (slice(None), columns)],
                        landing.at[step - 1] if axis == "z" else landing,
                        SLOTS[(route, 3 - stage, step)],
                        slot,
                        partner(axis, step),
                    )
                )
        return found

    def add(self, chunk, stage):
        core, x, y, z = place()
        slot = lax.rem(chunk, DEPTH)
        wide = jnp.float32
        if stage == 0:
            mine, theirs, pair = (self.work[k] for k in ("mine", "theirs", "pair"))

            def one(which, carry):
                a, b, c = which // 4, lax.rem(which // 2, 2), lax.rem(which, 2)
                pair[slot, a, b, c] = (
                    mine[slot, a, b, c].astype(wide) + theirs[slot, a, b, c].astype(wide)
                ).astype(pair.dtype)
                return carry

            lax.fori_loop(0, 16, one, 0)
            return
        at = {"x": x, "y": y, "z": z}
        for route, (gather_order, first, width) in enumerate(ROUTES):
            order = gather_order[::-1]
            axis = order[stage - 1]
            left = [name for name in "zyx" if name not in order[: stage - 1]]
            if stage == 1:
                held, columns = self.work["pair"], slice(first, first + width)
            else:
                held, columns = self.work["held", route, stage - 1], slice(None)
            index = tuple(at[axis] if name == axis else slice(None) for name in left)
            value = held[(slot,) + index + (slice(None), columns)].astype(wide)
            landing = self.work["land", route, stage]
            if axis == "z":
                for step in (1, 2, 3):
                    value = value + landing[slot, step - 1].astype(wide)
            else:
                value = value + landing[slot].astype(wide)
            if stage == 3:
                self.work["final"][slot, :, first : first + width] = value
            else:
                kept = self.work["held", route, stage]
                kept[slot] = value.astype(kept.dtype)

    def round(self, number):
        for stage in range(5):
            chunk = number - LAG * stage - LAG

            def finish(chunk=chunk, stage=stage):
                for copy in self.copies(chunk, stage):
                    copy.wait()
                if stage == 0:
                    self.load(chunk).wait()
                if stage == 4:
                    self.store(chunk).wait()
                else:
                    self.add(chunk, stage)

            when_in(chunk, self.count, finish)
        for stage in range(5):
            chunk = number - LAG * stage

            def begin(chunk=chunk, stage=stage):
                for copy in self.copies(chunk, stage):
                    copy.start()
                if stage == 0:
                    self.load(chunk).start()
                if stage == 4:
                    self.store(chunk).start()

            when_in(chunk, self.count, begin)


def scatter_scratch():
    low = jnp.bfloat16
    shapes = {
        "mine": ((4, 2, 2, BLK, D), low),
        "theirs": ((4, 2, 2, BLK, D), low),
        "pair": ((4, 2, 2, BLK, D), low),
        "final": ((BLK, D), jnp.float32),
    }
    size = {"z": 4, "y": 2, "x": 2}
    for route, (gather_order, first, width) in enumerate(ROUTES):
        order = gather_order[::-1]
        for stage in (1, 2, 3):
            axis = order[stage - 1]
            left = tuple(size[n] for n in "zyx" if n not in order[:stage])
            steps = (3,) if axis == "z" else ()
            shapes["land", route, stage] = (steps + left + (BLK, width), low)
            if stage < 3:
                shapes["held", route, stage] = (left + (BLK, width), low)
    return shapes


def scatter_kernel(count, names, partial, total, send, recv, local, *buffers):
    greet()
    rounds = Scatter(
        partial, total, dict(zip(names, buffers)), send, recv, local, count
    )

    def body(number, carry):
        rounds.round(number)
        return carry

    lax.fori_loop(0, rounds.rounds, body, 0)


def scatter(partial):
    rows = partial.shape[3]
    shapes = scatter_scratch()
    return pl.pallas_call(
        functools.partial(scatter_kernel, rows // PAIR, tuple(shapes)),
        out_shape=jax.ShapeDtypeStruct((rows, D), jnp.float32),
        in_specs=[pl.BlockSpec(memory_space=pl.ANY)],
        out_specs=pl.BlockSpec(memory_space=pl.ANY),
        scratch_shapes=[
            pltpu.SemaphoreType.DMA((SLOT_COUNT, DEPTH)),
            pltpu.SemaphoreType.DMA((SLOT_COUNT, DEPTH)),
            pltpu.SemaphoreType.DMA((2, DEPTH)),
        ]
        + [pltpu.VMEM((DEPTH,) + s, t) for s, t in shapes.values()],
        compiler_params=pltpu.CompilerParams(
            collective_id=1, has_side_effects=True, vmem_limit_bytes=48 * 2**20
        ),
        name="sum_gradients",
    )(partial)


NORM_EPS = 1e-12
MASKED = -1e30


def norm_rows(resid, gain, shift):
    average = jnp.mean(resid, axis=-1, keepdims=True)
    centered = resid - average
    spread = jnp.mean(centered * centered, axis=-1, keepdims=True)
    return centered * lax.rsqrt(spread + NORM_EPS) * gain + shift


def gelu_exact(values):
    return jax.nn.gelu(values, approximate=False)


def split_kinds(rows, short_count):
    cut = short_count * SHORT
    short_part = rows[:cut].reshape((short_count, SHORT) + rows.shape[1:])
    long_part = rows[cut:].reshape((-1, LONG) + rows.shape[1:])
    return (short_part, long_part)


def join_kinds(short_part, long_part):
    short_flat = short_part.reshape((-1,) + short_part.shape[2:])
    long_flat = long_part.reshape((-1,) + long_part.shape[2:])
    return jnp.concatenate([short_flat, long_flat], axis=0)


def attend_kind(packed, lengths):
    query_rows = packed[:, :, 0]
    key_rows = packed[:, :, 1]
    value_rows = packed[:, :, 2]
    score_scale = query_rows.shape[-1] ** (-0.5)
    scores = (
        jnp.einsum("bqhd,bkhd->bhqk", query_rows, key_rows, preferred_element_type=jnp.float32)
        * score_scale
    )
    visible = jnp.arange(key_rows.shape[1])[None, :] < lengths[:, None]
    scores = jnp.where(visible[:, None, None, :], scores, MASKED)
    highest = jnp.max(scores, axis=-1, keepdims=True)
    exponentials = jnp.exp(scores - highest)
    probabilities = exponentials / jnp.sum(exponentials, axis=-1, keepdims=True)
    context = jnp.einsum(
        "bhqk,bkhd->bqhd",
        probabilities.astype(jnp.bfloat16),
        value_rows,
        preferred_element_type=jnp.float32,
    )
    return (context, probabilities)


def attend_back(packed, probabilities, d_context):
    query_rows = packed[:, :, 0]
    key_rows = packed[:, :, 1]
    value_rows = packed[:, :, 2]
    score_scale = query_rows.shape[-1] ** (-0.5)
    d_probs = jnp.einsum(
        "bqhd,bkhd->bhqk", d_context, value_rows, preferred_element_type=jnp.float32
    )
    d_values = jnp.einsum(
        "bhqk,bqhd->bkhd",
        probabilities.astype(jnp.bfloat16),
        d_context,
        preferred_element_type=jnp.float32,
    )
    inner = jnp.sum(d_probs * probabilities, axis=-1, keepdims=True)
    d_scores = (probabilities * (d_probs - inner)).astype(jnp.bfloat16)
    d_queries = (
        jnp.einsum("bhqk,bkhd->bqhd", d_scores, key_rows, preferred_element_type=jnp.float32)
        * score_scale
    )
    d_keys = (
        jnp.einsum("bhqk,bqhd->bkhd", d_scores, query_rows, preferred_element_type=jnp.float32)
        * score_scale
    )
    return jnp.stack([d_queries, d_keys, d_values], axis=2)


def layer_forward(inputs, weights, qry_len, psg_len):
    w_qkv, w_o, w_in, w_out, bias_rows, gain_rows, in_bias = weights
    bias_float = bias_rows.astype(jnp.float32)
    gain_float = gain_rows.astype(jnp.float32)
    row_count = inputs.shape[0]
    inputs_low = inputs.astype(jnp.bfloat16)
    qkv_bias = jnp.concatenate([bias_float[0], jnp.zeros_like(bias_float[0]), bias_float[1]])
    packed = (jnp.dot(inputs_low, w_qkv, preferred_element_type=jnp.float32) + qkv_bias).astype(
        jnp.bfloat16
    )
    packed = packed.reshape(row_count, 3, H, HD)
    short_pack, long_pack = split_kinds(packed, qry_len.shape[0])
    short_context, short_softmax = attend_kind(short_pack, qry_len)
    long_context, long_softmax = attend_kind(long_pack, psg_len)
    context = join_kinds(short_context, long_context).reshape(row_count, -1).astype(jnp.bfloat16)
    attended = jnp.dot(context, w_o, preferred_element_type=jnp.float32) + bias_float[2]
    first_resid = inputs + attended
    first_norm = norm_rows(first_resid, gain_float[0], bias_float[3])
    first_low = first_norm.astype(jnp.bfloat16)
    upward = jnp.dot(first_low, w_in, preferred_element_type=jnp.float32) + in_bias.astype(
        jnp.float32
    )
    active_low = gelu_exact(upward).astype(jnp.bfloat16)
    second_resid = first_norm + (
        jnp.dot(active_low, w_out, preferred_element_type=jnp.float32) + bias_float[4]
    )
    outputs = norm_rows(second_resid, gain_float[1], bias_float[5])
    kept = (
        inputs_low,
        packed,
        short_softmax,
        long_softmax,
        context,
        first_resid,
        first_low,
        upward,
        active_low,
        second_resid,
    )
    return (outputs, kept)


def layer_backward(d_outputs, weights, kept, short_count):
    w_qkv, w_o, w_in, w_out, bias_rows, gain_rows, in_bias = weights
    (
        inputs_low,
        packed,
        short_softmax,
        long_softmax,
        context,
        first_resid,
        first_low,
        upward,
        active_low,
        second_resid,
    ) = kept
    bias_float = bias_rows.astype(jnp.float32)
    gain_float = gain_rows.astype(jnp.float32)
    row_count = d_outputs.shape[0]
    unused_second, pull_second = jax.vjp(norm_rows, second_resid, gain_float[1], bias_float[5])
    d_second, d_gain_two, d_shift_two = pull_second(d_outputs)
    d_down_low = d_second.astype(jnp.bfloat16)
    grad_out = jnp.dot(active_low.T, d_down_low, preferred_element_type=jnp.float32)
    d_active = jnp.dot(d_down_low, w_out.T, preferred_element_type=jnp.float32)
    unused_gelu, pull_gelu = jax.vjp(gelu_exact, upward)
    d_upward = pull_gelu(d_active)[0]
    d_up_low = d_upward.astype(jnp.bfloat16)
    grad_in = jnp.dot(first_low.T, d_up_low, preferred_element_type=jnp.float32)
    d_first_norm = d_second + jnp.dot(d_up_low, w_in.T, preferred_element_type=jnp.float32)
    unused_first, pull_first = jax.vjp(norm_rows, first_resid, gain_float[0], bias_float[3])
    d_first, d_gain_one, d_shift_one = pull_first(d_first_norm)
    d_att_low = d_first.astype(jnp.bfloat16)
    grad_o = jnp.dot(context.T, d_att_low, preferred_element_type=jnp.float32)
    d_context = jnp.dot(d_att_low, w_o.T, preferred_element_type=jnp.float32).astype(jnp.bfloat16)
    d_context = d_context.reshape(row_count, H, HD)
    short_pack, long_pack = split_kinds(packed, short_count)
    short_dctx, long_dctx = split_kinds(d_context, short_count)
    short_dpack = attend_back(short_pack, short_softmax, short_dctx)
    long_dpack = attend_back(long_pack, long_softmax, long_dctx)
    d_packed_low = join_kinds(short_dpack, long_dpack).reshape(row_count, -1).astype(jnp.bfloat16)
    grad_qkv = jnp.dot(inputs_low.T, d_packed_low, preferred_element_type=jnp.float32)
    d_inputs = d_first + jnp.dot(d_packed_low, w_qkv.T, preferred_element_type=jnp.float32)
    width = d_first.shape[1]
    column_sums = jnp.sum(d_packed_low.astype(jnp.float32), axis=0)
    bias_grads = jnp.stack(
        [
            column_sums[:width],
            column_sums[2 * width :],
            jnp.sum(d_first, axis=0),
            d_shift_one,
            jnp.sum(d_second, axis=0),
            d_shift_two,
        ]
    )
    gain_grads = jnp.stack([d_gain_one, d_gain_two])
    in_bias_grad = jnp.sum(d_upward, axis=0)
    return (d_inputs, (grad_qkv, grad_o, grad_in, grad_out, bias_grads, gain_grads, in_bias_grad))


def pack_own(w_qkv, w_o, w_in, w_out, biases, gains, in_bias):
    layers, part = w_qkv.shape[0], w_qkv.shape[1]
    pieces = []
    for layer in range(layers):
        for weight in (w_qkv[layer], w_o[layer], w_in[layer]):
            panels = weight.reshape(part, -1, D).transpose(1, 0, 2)
            pieces.append(panels.reshape(-1, D))
        pieces.append(w_out[layer])
    small = jnp.concatenate([biases.reshape(-1), gains.reshape(-1), in_bias.reshape(-1)])
    block = PAIR * D
    small = jnp.pad(small, (0, -small.shape[0] % block))
    pieces.append(small.reshape(-1, D))
    return jnp.concatenate(pieces, axis=0)


def small_parts(rows, parts, layers, part, hidden_part):
    flat = rows.reshape(parts, -1)
    cuts = (layers * 6 * part, layers * 8 * part, layers * (8 * part + hidden_part))
    biases = flat[:, : cuts[0]].reshape(parts, layers, 6, part)
    gains = flat[:, cuts[0] : cuts[1]].reshape(parts, layers, 2, part)
    in_bias = flat[:, cuts[1] : cuts[2]].reshape(parts, layers, hidden_part)
    return (
        biases.transpose(1, 2, 0, 3).reshape(layers, 6, -1),
        gains.transpose(1, 2, 0, 3).reshape(layers, 2, -1),
        in_bias.transpose(1, 0, 2).reshape(layers, -1),
    )


def layer_rows(part):
    return (0, 3 * part, 4 * part, 8 * part, 12 * part)


def shards(
    hidden, qry_len, psg_len, qry_grad, psg_grad, w_qkv, w_o, w_in, w_out, biases, gains, in_bias, parts, near
):
    layers, part, hidden_part = w_qkv.shape[0], w_qkv.shape[1], w_out.shape[1]
    cuts = layer_rows(part)
    short_count = qry_len.shape[0]
    own = pack_own(w_qkv, w_o, w_in, w_out, biases, gains, in_bias)
    rows = own.shape[0]
    if near:
        whole = gather(own).reshape(parts, rows, D)
    else:
        whole = lax.all_gather(own, "fsdp", axis=0)
    all_biases, all_gains, all_in_bias = small_parts(
        whole[:, layers * cuts[4] :], parts, layers, part, hidden_part
    )

    def unpanel(block):
        count = block.shape[1] // part
        return block.reshape(parts, count, part, D).transpose(0, 2, 1, 3).reshape(D, count * D)

    inputs = hidden.astype(jnp.float32)
    kept_each, weights_each = [], []
    for layer in range(layers):
        block = whole[:, layer * cuts[4] : (layer + 1) * cuts[4]]
        weights = (
            unpanel(block[:, cuts[0] : cuts[1]]),
            unpanel(block[:, cuts[1] : cuts[2]]),
            unpanel(block[:, cuts[2] : cuts[3]]),
            block[:, cuts[3] :].reshape(-1, D),
            all_biases[layer],
            all_gains[layer],
            all_in_bias[layer],
        )
        inputs, kept = layer_forward(inputs, weights, qry_len, psg_len)
        kept_each.append(kept)
        weights_each.append(weights)
    short_live = (jnp.arange(SHORT)[None, :] < qry_len[:, None]).astype(
        jnp.float32
    ) / qry_len.astype(jnp.float32)[:, None]
    long_live = (jnp.arange(LONG)[None, :] < psg_len[:, None]).astype(jnp.float32) / psg_len.astype(
        jnp.float32
    )[:, None]
    d_inputs = join_kinds(
        short_live[:, :, None] * qry_grad[:, None, :], long_live[:, :, None] * psg_grad[:, None, :]
    )

    def panel(grad):
        count = grad.shape[1] // D
        return grad.reshape(parts, part, count, D).transpose(0, 2, 1, 3).reshape(parts, -1, D)

    grads_each = [None] * layers
    for layer in range(layers - 1, -1, -1):
        d_inputs, grads_each[layer] = layer_backward(
            d_inputs, weights_each[layer], kept_each[layer], short_count
        )
    pieces = []
    for grads in grads_each:
        pieces += [panel(g.astype(jnp.bfloat16)) for g in grads[:3]]
        pieces.append(grads[3].astype(jnp.bfloat16).reshape(parts, -1, D))
    small = [
        jnp.stack([g[which] for g in grads_each])
        .reshape(layers, -1, parts, size)
        .transpose(2, 0, 1, 3)
        .reshape(parts, -1)
        for which, size in ((4, part), (5, part), (6, hidden_part))
    ]
    small = jnp.concatenate(small, axis=1).astype(jnp.bfloat16)
    small = jnp.pad(small, ((0, 0), (0, (rows - layers * cuts[4]) * D - small.shape[1])))
    pieces.append(small.reshape(parts, -1, D))
    partial = jnp.concatenate(pieces, axis=1)
    if near:
        total = scatter(partial.reshape(4, 2, 2, rows, D))
    else:
        total = lax.psum_scatter(partial.astype(jnp.float32), "fsdp", scatter_dimension=0)
        total = lax.psum(total, "rep")
    grads = total[: layers * cuts[4]].reshape(layers, cuts[4], D)

    def unpack(first, last):
        block = grads[:, first:last].reshape(layers, -1, part, D)
        return block.transpose(0, 2, 1, 3).reshape(layers, part, -1)

    small = total[layers * cuts[4] :].reshape(1, -1)
    d_biases, d_gains, d_in_bias = small_parts(small, 1, layers, part, hidden_part)
    return (
        inputs.astype(jnp.bfloat16),
        d_inputs.astype(jnp.bfloat16),
        unpack(cuts[0], cuts[1]),
        unpack(cuts[1], cuts[2]),
        unpack(cuts[2], cuts[3]),
        grads[:, cuts[3] :],
        d_biases,
        d_gains,
        d_in_bias,
    )


def solution(mesh):
    placed = (
        P(("rep", "fsdp"), None),
        P(("rep", "fsdp")),
        P(("rep", "fsdp")),
        P(("rep", "fsdp"), None),
        P(("rep", "fsdp"), None),
        P(None, "fsdp", None),
        P(None, "fsdp", None),
        P(None, "fsdp", None),
        P(None, "fsdp", None),
        P(None, None, "fsdp"),
        P(None, None, "fsdp"),
        P(None, "fsdp"),
    )
    parts = mesh.shape["fsdp"]
    near = parts == 16 and mesh.shape["rep"] == 2
    return jax.shard_map(
        functools.partial(shards, parts=parts, near=near),
        mesh=mesh,
        in_specs=placed,
        out_specs=(
            P(("rep", "fsdp"), None),
            P(("rep", "fsdp"), None),
            P(None, "fsdp", None),
            P(None, "fsdp", None),
            P(None, "fsdp", None),
            P(None, "fsdp", None),
            P(None, None, "fsdp"),
            P(None, None, "fsdp"),
            P(None, "fsdp"),
        ),
        check_vma=False,
    )
```

```python
import functools

import jax
import jax.numpy as jnp
from jax import lax
from jax.experimental import pallas as pl
from jax.experimental.pallas import tpu as pltpu
from jax.sharding import PartitionSpec as P

MESH = pl.DeviceIdType.MESH
LOW, WIDE = jnp.bfloat16, jnp.float32
D = 768
HALF = 64
SHORT = 128
LONG = 512
PAIRS = D // 128
NORM_EPS = 1e-12
MASKED = -1e30
VMEM_BYTES = 60 * 2**20
NN = (((1,), (0,)), ((), ()))
NT = (((1,), (1,)), ((), ()))
TN = (((0,), (0,)), ((), ()))

BLK = 16
PAIR = 2 * BLK
LAG = 2
DEPTH = 4
X, Y, Z, CORE = 0, 1, 2, 3
SIZES = {X: 2, Y: 2, Z: 4}
ROUTES = (
    ((X, Z, Y), 0, 128),
    ((Y, Z, X), 128, 128),
    ((Z, X, Y), 256, 256),
    ((Z, Y, X), 512, 256),
)
MINE, THEIRS, SUMMED, FINAL, LAND, HELD = range(6)

Q_AT, K_AT, V_AT, O_AT, IN_AT, OUT_AT, PANELS = 0, 1, 2, 3, 4, 8, 12
PART = D // 16
LAYER_CHUNKS = PANELS * PART // PAIR
GAIN_ROW, HIDDEN_ROW, SMALL_ROWS = 12, 16, 24


def steps_of(axis):
    return (1, 2, 3) if axis == Z else (1,)


class Place:
    def __init__(self):
        core = lax.axis_index("rep")
        spot = lax.axis_index("fsdp")
        x, y, z = lax.rem(spot, 2), lax.rem(spot // 2, 2), spot // 4
        self.core = core
        self.at = {X: x, Y: y, Z: z}
        self.to = {
            (CORE, 1): (1 - core, spot),
            (X, 1): (core, spot + 1 - 2 * x),
            (Y, 1): (core, spot + 2 - 4 * y),
        }
        self.next_z = {}
        for step in (1, 2, 3):
            other = lax.rem(z + step, 4)
            self.next_z[step] = other
            self.to[Z, step] = (core, other * 4 + y * 2 + x)

    def greet(self):
        barrier = pltpu.get_barrier_semaphore()
        for device in self.to.values():
            pl.semaphore_signal(barrier, inc=1, device_id=device, device_id_type=MESH)
        pl.semaphore_wait(barrier, len(self.to))


SLOTS = {}
for _route, (_order, _first, _width) in enumerate(ROUTES):
    for _stage in range(3):
        for _step in steps_of(_order[_stage]):
            SLOTS[_route, _stage, _step] = len(SLOTS)
CORE_SLOT = len(SLOTS)
FINAL_SLOT = CORE_SLOT + 1
SLOT_COUNT = CORE_SLOT + 2


def when_in(chunk, count, work):
    pl.when(jnp.logical_and(chunk >= 0, chunk < count))(work)


class Rounds:
    stages = 0

    def __init__(self, place, send, recv, local, count):
        self.place, self.send, self.recv, self.local, self.count = place, send, recv, local, count
        self.rounds = count + self.stages * LAG

    def remote(self, source, target, index, slot, partner):
        return pltpu.make_async_remote_copy(
            src_ref=source,
            dst_ref=target,
            send_sem=self.send.at[index, slot],
            recv_sem=self.recv.at[index, slot],
            device_id=self.place.to[partner],
            device_id_type=MESH,
        )

    def rows(self, chunk, core):
        return pl.ds(pl.multiple_of(self.spot(chunk) * PAIR + core * BLK, BLK), BLK)

    def finish(self, number):
        for stage in range(self.stages):
            chunk = number - LAG * stage - LAG

            def work(chunk=chunk, stage=stage):
                for copy in self.copies(chunk, stage):
                    copy.wait()
                self.finished(chunk, stage)

            when_in(chunk, self.count, work)

    def begin(self, number):
        for stage in range(self.stages):
            chunk = number - LAG * stage

            def work(chunk=chunk, stage=stage):
                for copy in self.copies(chunk, stage):
                    copy.start()

            when_in(chunk, self.count, work)

    def round(self, number):
        self.finish(number)
        self.begin(number)

    def drain(self, begin):
        def body(step, carry):
            number = begin + 2 * step
            self.finish(number)
            self.finish(number + 1)
            self.begin(number)
            self.begin(number + 1)
            return carry

        lax.fori_loop(0, (self.rounds - begin + 1) // 2, body, 0)

    def finished(self, chunk, stage):
        pass


class Gather(Rounds):
    stages = 4

    def __init__(self, own, whole, *rest):
        super().__init__(*rest)
        self.own, self.whole = own, whole

    def spot(self, chunk):
        return lax.rem(chunk + self.count - 1, self.count)

    def copies(self, chunk, stage):
        at = self.place.at
        slot = lax.rem(chunk, DEPTH)
        rows = self.rows(chunk, self.place.core)
        if stage == 3:
            part = self.whole.at[:, :, :, rows, :]
            return [self.remote(part, part, CORE_SLOT, slot, (CORE, 1))]
        found = []
        if stage == 0:
            found.append(
                pltpu.make_async_copy(
                    self.own.at[rows, :],
                    self.whole.at[at[Z], at[Y], at[X], rows, :],
                    self.local.at[0, slot],
                )
            )
        for route, (order, first, width) in enumerate(ROUTES):
            axis, done = order[stage], order[:stage]
            columns = pl.ds(first, width)
            if stage == 0:
                source = self.own.at[rows, columns]
                part = self.whole.at[at[Z], at[Y], at[X], rows, columns]
            else:
                spans = [
                    pl.ds(0, SIZES[name]) if name in done else pl.ds(at[name], 1)
                    for name in (Z, Y, X)
                ]
                source = part = self.whole.at[spans[0], spans[1], spans[2], rows, columns]
            for step in steps_of(axis):
                index = SLOTS[route, stage, step]
                found.append(self.remote(source, part, index, slot, (axis, step)))
        return found


class Scatter(Rounds):
    stages = 5

    def __init__(self, partial, total, work, *rest):
        super().__init__(*rest)
        self.partial, self.total, self.work = partial, total, work

    def spot(self, chunk):
        return lax.rem(2 * self.count - 2 - chunk, self.count)

    def copies(self, chunk, stage):
        core, at = self.place.core, self.place.at
        slot = lax.rem(chunk, DEPTH)
        rows = self.rows(chunk, core)
        if stage == 0:
            theirs = self.partial.at[:, :, :, self.rows(chunk, 1 - core), :]
            mine = pltpu.make_async_copy(
                self.partial.at[:, :, :, rows, :],
                self.work[MINE].at[slot],
                self.local.at[0, slot],
            )
            landing = self.work[THEIRS].at[slot]
            return [mine, self.remote(theirs, landing, CORE_SLOT, slot, (CORE, 1))]
        if stage == 4:
            source, target = self.work[FINAL].at[slot], self.total.at[rows, :]
            mine = pltpu.make_async_copy(source, target, self.local.at[1, slot])
            return [mine, self.remote(source, target, FINAL_SLOT, slot, (CORE, 1))]
        found = []
        for route, (gather_order, first, width) in enumerate(ROUTES):
            order = gather_order[::-1]
            axis, left = order[stage - 1], [n for n in (Z, Y, X) if n not in order[: stage - 1]]
            if stage == 1:
                held, columns = self.work[SUMMED].at[slot], pl.ds(first, width)
            else:
                held, columns = self.work[HELD, route, stage - 1].at[slot], slice(None)
            landing = self.work[LAND, route, stage].at[slot]
            for step in steps_of(axis):
                to = self.place.next_z[step] if axis == Z else 1 - at[axis]
                index = tuple(to if name == axis else slice(None) for name in left)
                found.append(
                    self.remote(
                        held.at[index + (slice(None), columns)],
                        landing.at[step - 1] if axis == Z else landing,
                        SLOTS[route, 3 - stage, step],
                        slot,
                        (axis, step),
                    )
                )
        return found

    def finished(self, chunk, stage):
        at = self.place.at
        slot = lax.rem(chunk, DEPTH)
        if stage == 0:
            self.work[SUMMED][slot] = self.work[MINE][slot] + self.work[THEIRS][slot]
        if stage in (0, 4):
            return
        for route, (gather_order, first, width) in enumerate(ROUTES):
            order = gather_order[::-1]
            axis, left = order[stage - 1], [n for n in (Z, Y, X) if n not in order[: stage - 1]]
            if stage == 1:
                held, columns = self.work[SUMMED], slice(first, first + width)
            else:
                held, columns = self.work[HELD, route, stage - 1], slice(None)
            index = tuple(at[axis] if name == axis else slice(None) for name in left)
            value = held[(slot,) + index + (slice(None), columns)]
            landing = self.work[LAND, route, stage]
            if axis == Z:
                value = value.astype(WIDE)
                for step in (1, 2, 3):
                    value = value + landing[slot, step - 1].astype(WIDE)
            elif stage == 3:
                value = value.astype(WIDE) + landing[slot].astype(WIDE)
            else:
                value = value + landing[slot]
            if stage == 3:
                self.work[FINAL][slot, :, first : first + width] = value
            else:
                self.work[HELD, route, stage][slot] = value.astype(LOW)


def scatter_scratch():
    shapes = {
        MINE: ((4, 2, 2, BLK, D), LOW),
        THEIRS: ((4, 2, 2, BLK, D), LOW),
        SUMMED: ((4, 2, 2, BLK, D), LOW),
        FINAL: ((BLK, D), WIDE),
    }
    for route, (gather_order, first, width) in enumerate(ROUTES):
        order = gather_order[::-1]
        for stage in (1, 2, 3):
            left = tuple(SIZES[n] for n in (Z, Y, X) if n not in order[:stage])
            steps = (3,) if order[stage - 1] == Z else ()
            shapes[LAND, route, stage] = (steps + left + (BLK, width), LOW)
            if stage < 3:
                shapes[HELD, route, stage] = (left + (BLK, width), LOW)
    return shapes


def advance(rounds, begin, end):
    if rounds is None:
        return

    def body(number, carry):
        rounds.round(number)
        return carry

    lax.fori_loop(begin, end, body, 0)


class Pending:
    def __init__(self, semaphores):
        self.semaphores, self.known, self.flying = semaphores, {}, {}

    def start(self, key, source, target):
        self.wait(key)
        at = self.known.setdefault(key, len(self.known))
        copy = pltpu.make_async_copy(source, target, self.semaphores.at[at])
        copy.start()
        self.flying[key] = copy

    def wait(self, *keys):
        for key in keys:
            copy = self.flying.pop(key, None)
            if copy is not None:
                copy.wait()

    def wait_all(self):
        self.wait(*list(self.flying))


def dot(left, right, numbers):
    return lax.dot_general(left, right, numbers, preferred_element_type=WIDE)


def norm_parts(resid):
    average = jnp.mean(resid, axis=-1, keepdims=True)
    centered = resid - average
    spread = jnp.mean(centered * centered, axis=-1, keepdims=True)
    scale = lax.rsqrt(spread + NORM_EPS)
    return centered * scale, scale


def column_sum(value):
    return jnp.sum(value, axis=0, keepdims=True)


def lanes_of(pair):
    return pl.ds(pl.multiple_of(pair * 128, 128), 128)


def sequences(qry_len, psg_len):
    return (
        (2 * SHORT, LONG, psg_len[0]),
        (0, SHORT, qry_len[0]),
        (SHORT, SHORT, qry_len[1]),
    )


def rows_in(size, work):
    def body(step, carry):
        work(pl.ds(pl.multiple_of(step * size, size), size))
        return carry

    lax.fori_loop(0, D // size, body, 0)


def section(ref, layer, first, panels):
    return ref.at[:, :, :, pl.ds((layer * PANELS + first) * PART, panels * PART), :]


def matrix(ref):
    return ref[...].reshape(-1, D)


FORWARD_BLOCK = 512
BACKWARD_BLOCK = 512


def place_lanes(shape):
    lane = lax.broadcasted_iota(jnp.int32, shape, 1)
    return lane // HALF, lane % HALF


def dead_rows(length, live):
    row = lax.broadcasted_iota(jnp.int32, (length, 128), 0)
    return jnp.where(row < live, 0.0, MASKED).astype(LOW)


def three_parts(value):
    high = value.astype(LOW)
    rest = value - high.astype(WIDE)
    middle = rest.astype(LOW)
    return high, middle, (rest - middle.astype(WIDE)).astype(LOW)


def attend(pair, packed, extended, context, spans):
    lanes = lanes_of(pair)
    for first, length, live in spans:
        size = min(length, FORWARD_BLOCK)
        head, lane = place_lanes((length, 128))
        keys = packed[1, first : first + length, lanes]
        values = packed[2, first : first + length, lanes]
        dead = jnp.where(lane == 0, dead_rows(length, live), jnp.zeros((), LOW))
        my_keys = [jnp.where(head == which, keys, dead) for which in range(2)]
        my_values = [jnp.where(head == which, values, jnp.ones((), LOW)) for which in range(2)]
        head, lane = place_lanes((size, 128))
        unit = jnp.where(lane == 0, 1.0, 0.0).astype(LOW)
        for start in range(first, first + length, size):
            queries = packed[0, start : start + size, lanes] * jnp.array(HALF**-0.5, LOW)
            found = []
            for which in range(2):
                mine = jnp.where(head == which, queries, unit)
                scores = dot(mine, my_keys[which], NT)
                highest = jnp.max(scores, axis=-1, keepdims=True)
                raised = jnp.exp(scores - highest).astype(LOW)
                result = dot(raised, my_values[which], NN)
                found.append(result / pltpu.roll(result, HALF, axis=1))
                parts = three_parts(-(highest + jnp.log(result)))
                for at, value in enumerate(parts):
                    unit_at = jnp.logical_and(head != which, lane == at + 1)
                    mine = jnp.where(unit_at, value, mine)
                extended[2 * pair + which, start : start + size, :] = mine
            context[start : start + size, lanes] = jnp.where(
                head == 0, found[0], found[1]
            ).astype(LOW)


def attend_back(pair, packed, extended, context, d_context, d_packed, d_keys, d_values, spans):
    lanes = lanes_of(pair)
    for first, length, live in spans:
        size = min(length, BACKWARD_BLOCK)
        head, lane = place_lanes((length, 128))
        keys = packed[1, first : first + length, lanes]
        values = packed[2, first : first + length, lanes]
        blank = jnp.zeros_like(keys)
        ones = jnp.where(jnp.logical_and(lane >= 1, lane <= 3), 1.0, 0.0).astype(LOW)
        dead = jnp.where(lane == 0, dead_rows(length, live), ones)
        only_keys = [jnp.where(head == which, keys, blank) for which in range(2)]
        my_keys = [jnp.where(head == which, keys, dead) for which in range(2)]
        my_values = [jnp.where(head == which, values, ones) for which in range(2)]
        both_keys = jnp.concatenate(only_keys, axis=0)
        head, lane = place_lanes((size, 128))
        blank = jnp.zeros((size, 128), LOW)
        for start in range(first, first + length, size):
            upstream = d_context[start : start + size, lanes]
            product = upstream.astype(WIDE) * context[start : start + size, lanes].astype(WIDE)
            all_probs, all_scores, all_queries, all_upstream = [], [], [], []
            for which in range(2):
                queries = extended[2 * pair + which, start : start + size, :]
                mine = jnp.where(head == which, upstream, blank)
                all_queries.append(jnp.where(head == which, queries, blank))
                all_upstream.append(mine)
                inner = jnp.sum(jnp.where(head == which, product, 0.0), axis=1, keepdims=True)
                parts = three_parts(jnp.broadcast_to(-inner, (size, 128)))
                for at, value in enumerate(parts):
                    unit_at = jnp.logical_and(head != which, lane == at + 1)
                    mine = jnp.where(unit_at, value, mine)
                probs = jnp.exp(dot(my_keys[which], queries, NT))
                d_scores = probs * dot(my_values[which], mine, NT)
                all_probs.append(probs.astype(LOW))
                all_scores.append(d_scores.astype(LOW))
            d_packed[0, start : start + size, lanes] = (
                dot(jnp.concatenate(all_scores, axis=0), both_keys, TN) * (HALF**-0.5)
            ).astype(LOW)
            k_now = dot(
                jnp.concatenate(all_scores, axis=1), jnp.concatenate(all_queries, axis=0), NN
            )
            v_now = dot(
                jnp.concatenate(all_probs, axis=1), jnp.concatenate(all_upstream, axis=0), NN
            )
            if size < length:
                if start > first:
                    k_now = d_keys[...] + k_now
                    v_now = d_values[...] + v_now
                if start + size < first + length:
                    d_keys[...] = k_now
                    d_values[...] = v_now
                    continue
            d_packed[1, first : first + length, lanes] = k_now.astype(LOW)
            d_packed[2, first : first + length, lanes] = v_now.astype(LOW)


KEPT_LOW, PACKED, CONTEXT, EXTENDED, FIRST_LOW, ACTIVE, SLOPE, FIRST_RESID, SECOND_RESID = range(9)
KEPT = (
    ((D, D), LOW),
    ((3, D, D), LOW),
    ((D, D), LOW),
    ((2 * PAIRS, D, 128), LOW),
    ((D, D), LOW),
    ((4, D, D), LOW),
    ((4, D, D), LOW),
    ((D, D), WIDE),
    ((D, D), WIDE),
)
WEIGHT, READY, SMALL, OWN = 10, 11, 12, 13


def forward_kernel(near, layers, count, *refs):
    hidden, qry_len, psg_len = refs[:3]
    if near:
        w_qkv, w_o, w_in, w_out, small_own, whole = refs[3:9]
        refs = refs[9:]
    else:
        whole, refs = refs[3], refs[4:]
    mixed, kept, refs = refs[0], refs[1 : 1 + len(KEPT)], refs[1 + len(KEPT) :]
    (state, total, resid, low, packed, context, extended, first_low, active, slope) = refs[:10]
    (attention_weights, in_weights, out_weights, small, params, semaphores) = refs[10:16]
    rounds = None
    copies = Pending(semaphores)
    if near:
        place, own = Place(), refs[16]
        for layer in range(layers):
            base = layer * PANELS
            blocks = [(w_qkv, 3, Q_AT), (w_o, 1, O_AT), (w_in, 4, IN_AT)]
            for ref, panels, first in blocks:
                for panel in range(panels):
                    copies.start(
                        (OWN, layer, first + panel),
                        ref.at[layer, :, pl.ds(panel * D, D)],
                        own.at[pl.ds((base + first + panel) * PART, PART), :],
                    )
            copies.start(
                (OWN, layer, OUT_AT),
                w_out.at[layer],
                own.at[pl.ds((base + OUT_AT) * PART, 4 * PART), :],
            )
        copies.start((OWN, layers, 0), small_own, own.at[pl.ds(layers * PANELS * PART, PAIR), :])
        place.greet()
        copies.wait_all()
        rounds = Gather(own, whole, place, *refs[17:20], count)
    spans = sequences(qry_len, psg_len)

    def keep(which, layer, ref, panel=None):
        target = kept[which].at[layer] if panel is None else kept[which].at[layer, panel]
        copies.start((which, panel), ref, target)

    def fetch(panel, layer, target):
        copies.start((WEIGHT, panel), section(whole, layer, panel, 1), target)

    spent = [0]

    def run(end):
        if near:
            end = min(end, rounds.rounds)
        if end > spent[0]:
            advance(rounds, spent[0], end)
            spent[0] = end

    run(9)
    copies.start(SMALL, whole.at[:, :, :, pl.ds(layers * PANELS * PART, PAIR), :], small)
    state[...] = hidden[...].astype(WIDE)
    low[...] = hidden[...]
    keep(KEPT_LOW, 0, low)
    copies.wait(SMALL)
    params[...] = jnp.sum(small[...].astype(WIDE), axis=(0, 1, 2))

    def row(at):
        return params[pl.ds(at, 1), :]

    run(14)
    for panel in (Q_AT, K_AT, V_AT):
        fetch(panel, 0, attention_weights.at[panel])
    for layer in range(layers):
        base = LAYER_CHUNKS * layer
        copies.wait((PACKED, None))
        for panel in (Q_AT, K_AT, V_AT):
            copies.wait((WEIGHT, panel))
            value = dot(low[...], matrix(attention_weights.at[panel]), NN)
            if panel != K_AT:
                value = value + row(6 * layer + (0 if panel == Q_AT else 1))
            packed[panel] = value.astype(LOW)
            run(base + 15 + panel)
        keep(PACKED, layer, packed)
        fetch(O_AT, layer, attention_weights.at[O_AT])
        fetch(IN_AT, layer, in_weights.at[0])
        copies.wait((CONTEXT, None), (EXTENDED, None))

        def heads(pair, carry):
            attend(pair, packed, extended, context, spans)
            advance(rounds, base + 17 + pair // 2, base + 17 + (pair + 1) // 2)
            return carry

        lax.fori_loop(0, PAIRS, heads, 0)
        spent[0] = base + 20
        keep(CONTEXT, layer, context)
        keep(EXTENDED, layer, extended)
        fetch(IN_AT + 1, layer, in_weights.at[1])
        copies.wait((WEIGHT, O_AT), (SECOND_RESID, None))
        total[...] = dot(context[...], matrix(attention_weights.at[O_AT]), NN)
        run(base + 21)
        copies.wait((FIRST_RESID, None), (FIRST_LOW, None))

        def normalise_first(rows):
            value = state[rows, :] + (total[rows, :] + row(6 * layer + 2))
            resid[rows, :] = value
            norm = norm_parts(value)[0] * row(GAIN_ROW + 2 * layer) + row(6 * layer + 3)
            first_low[rows, :] = norm.astype(LOW)
            total[rows, :] = norm + row(6 * layer + 4)

        rows_in(128, normalise_first)
        keep(FIRST_RESID, layer, resid)
        keep(FIRST_LOW, layer, first_low)
        for panel in range(4):
            copies.wait((WEIGHT, IN_AT + panel))
            copies.wait((ACTIVE, panel), (SLOPE, panel), (SLOPE, (panel + 2) % 4))

            def inward(rows):
                upward = dot(first_low[rows, :], matrix(in_weights.at[panel % 2]), NN)
                upward = upward + row(HIDDEN_ROW + 4 * layer + panel)
                share = 0.5 + 0.5 * lax.erf(upward * (0.5**0.5))
                bell = jnp.exp(upward * upward * -0.5) * 0.3989422804014327
                active[panel, rows, :] = (upward * share).astype(LOW)
                slope[panel % 2, rows, :] = (share + upward * bell).astype(LOW)

            rows_in(384, inward)
            keep(ACTIVE, layer, active.at[panel], panel)
            keep(SLOPE, layer, slope.at[panel % 2], panel)
            if panel < 2:
                fetch(IN_AT + panel + 2, layer, in_weights.at[panel])
            run(base + 22 + panel)
        run(base + 27)
        for panel in range(4):
            rows = pl.ds((layer * PANELS + OUT_AT) * PART, 4 * PART)
            copies.start(
                (WEIGHT, OUT_AT + panel), whole.at[panel, :, :, rows, :], out_weights.at[panel]
            )
        for panel in range(4):
            copies.wait((WEIGHT, OUT_AT + panel))
            total[...] += dot(active[panel], matrix(out_weights.at[panel]), NN)
            if layer + 1 < layers and panel % 2:
                run(base + 28 + panel // 2)
        if layer + 1 < layers:
            run(base + 32)
            for panel in (Q_AT, K_AT, V_AT):
                fetch(panel, layer + 1, attention_weights.at[panel])
        copies.wait((KEPT_LOW, None))

        def normalise_second(rows):
            norm = norm_parts(total[rows, :])[0]
            value = norm * row(GAIN_ROW + 2 * layer + 1) + row(6 * layer + 5)
            state[rows, :] = value
            low[rows, :] = value.astype(LOW)

        keep(SECOND_RESID, layer, total)
        rows_in(128, normalise_second)
        if layer == layers - 1:
            mixed[...] = low[...]
        else:
            keep(KEPT_LOW, layer + 1, low)
    copies.wait_all()


def vmem(*shape, dtype=LOW):
    return pltpu.VMEM(shape, dtype)


def places():
    return (
        pl.BlockSpec(memory_space=pltpu.VMEM),
        pl.BlockSpec(memory_space=pltpu.SMEM),
        pl.BlockSpec(memory_space=pl.ANY),
    )


def transfer_scratch():
    return [
        pltpu.SemaphoreType.DMA((SLOT_COUNT, DEPTH)),
        pltpu.SemaphoreType.DMA((SLOT_COUNT, DEPTH)),
        pltpu.SemaphoreType.DMA((2, DEPTH)),
    ]


def params_of(identity):
    extra = {}
    if identity is not None:
        extra = dict(collective_id=identity, has_side_effects=True)
    return pltpu.CompilerParams(vmem_limit_bytes=VMEM_BYTES, **extra)


def forward(hidden, qry_len, psg_len, sources, layers, near):
    here, scalars, far = places()
    rows = layers * PANELS * PART + PAIR
    outs = [jax.ShapeDtypeStruct((D, D), LOW)]
    outs += [jax.ShapeDtypeStruct((layers,) + s, t) for s, t in KEPT]
    specs = [here] + [far] * len(KEPT)
    if near:
        outs = [jax.ShapeDtypeStruct((4, 2, 2, rows, D), LOW)] + outs
        specs = [far] + specs
    panel = (4, 2, 2, PART, D)
    scratch = [
        vmem(D, D, dtype=WIDE),
        vmem(D, D, dtype=WIDE),
        vmem(D, D, dtype=WIDE),
        vmem(D, D),
        vmem(3, D, D),
        vmem(D, D),
        vmem(2 * PAIRS, D, 128),
        vmem(D, D),
        vmem(4, D, D),
        vmem(2, D, D),
        vmem(4, *panel),
        vmem(2, *panel),
        vmem(4, 2, 2, 4 * PART, D),
        vmem(4, 2, 2, PAIR, D),
        vmem(PAIR, D, dtype=WIDE),
        pltpu.SemaphoreType.DMA((64,)),
    ]
    if near:
        scratch += [vmem(rows, D)] + transfer_scratch()
    found = pl.pallas_call(
        functools.partial(forward_kernel, near, layers, rows // PAIR),
        out_shape=outs,
        in_specs=[here, scalars, scalars] + [far] * len(sources),
        out_specs=specs,
        scratch_shapes=scratch,
        compiler_params=params_of(0 if near else None),
        name="forward",
    )(hidden, qry_len, psg_len, *sources)
    if near:
        return found[0], found[1], found[2:]
    return sources[0], found[0], found[1:]


def backward_kernel(near, layers, count, names, *refs):
    qry_grad, psg_grad, qry_len, psg_len, whole = refs[:5]
    kept, refs = refs[5 : 5 + len(KEPT)], refs[5 + len(KEPT) :]
    partial, d_hidden, refs = refs[0], refs[1], refs[2:]
    if near:
        sums, refs = refs[0], refs[1:]
    targets, refs = dict(zip(HELD_BACK, refs)), refs[len(HELD_BACK) :]
    (slope, flow, d_low, d_context, d_packed, d_upward, attention_weights, in_weights) = refs[:8]
    (out_weights, ready, small, params, grads, d_keys, d_values, semaphores) = refs[8:16]
    rounds = None
    if near:
        place = Place()
        place.greet()
        work = dict(zip(names, refs[19:]))
        rounds = Scatter(partial, sums, work, place, *refs[16:19], count)
    copies = Pending(semaphores)
    spans = sequences(qry_len, psg_len)
    tail = layers * PANELS * PART

    def load(which, layer):
        copies.start(which, kept[which].at[layer], targets[which])

    def fetch(panel, layer, target):
        copies.start((WEIGHT, panel), section(whole, layer, panel, 1), target)

    def fetch_out(layer, panel):
        rows = pl.ds((layer * PANELS + OUT_AT) * PART, 4 * PART)
        copies.start(
            (WEIGHT, OUT_AT + panel), whole.at[panel, :, :, rows, :], out_weights.at[panel % 2]
        )

    def load_hidden(layer, panel):
        copies.start((SLOPE, panel % 2), kept[SLOPE].at[layer, panel], slope.at[panel % 2])
        fetch_out(layer, panel)
        fetch(IN_AT + panel, layer, in_weights.at[panel % 2])

    turn = [0]

    def deliver(value, target, shape):
        at = turn[0] % 4
        turn[0] += 1
        copies.wait((READY, at))
        ready[at] = value.astype(LOW)
        copies.start((READY, at), ready.at[at].reshape(shape), target)

    def pause(end):
        copies.wait(*[(READY, at) for at in range(4)])
        run(end)

    def deliver_panel(value, layer, panel):
        deliver(value, section(partial, layer, panel, 1), (4, 2, 2, PART, D))

    def row(at):
        return params[pl.ds(at, 1), :]

    copies.start(SMALL, whole.at[:, :, :, pl.ds(tail, PAIR), :], small)
    for which in (SECOND_RESID, ACTIVE):
        load(which, layers - 1)
    load_hidden(layers - 1, 3)
    for which in (FIRST_LOW, FIRST_RESID, CONTEXT, EXTENDED, PACKED, KEPT_LOW):
        load(which, layers - 1)
    grads[...] = jnp.zeros_like(grads)
    for at, (first, length, live) in enumerate(spans):
        upstream = psg_grad[...] if at == 0 else qry_grad[at - 1 : at, :]
        alive = lax.broadcasted_iota(jnp.int32, (length, D), 0) < live
        flow[first : first + length, :] = jnp.where(alive, upstream, 0.0) / live.astype(WIDE)
    copies.wait(SMALL)
    params[...] = jnp.sum(small[...].astype(WIDE), axis=(0, 1, 2))

    def norm_back(resid, gain, gain_row, shift_row, sum_row):
        def block(rows):
            norm, scale = norm_parts(resid[rows, :])
            upstream = flow[rows, :]
            grads[pl.ds(gain_row, 1), :] += column_sum(upstream * norm)
            grads[pl.ds(shift_row, 1), :] += column_sum(upstream)
            scaled = upstream * gain
            result = (
                scaled
                - jnp.mean(scaled, axis=-1, keepdims=True)
                - norm * jnp.mean(scaled * norm, axis=-1, keepdims=True)
            ) * scale
            grads[pl.ds(sum_row, 1), :] += column_sum(result)
            flow[rows, :] = result
            d_low[rows, :] = result.astype(LOW)

        rows_in(128, block)

    spent = [0]

    def run(end):
        if end > spent[0]:
            advance(rounds, spent[0], end)
            spent[0] = end

    for layer in range(layers - 1, -1, -1):
        base = LAYER_CHUNKS * (layers - 1 - layer)
        copies.wait(SECOND_RESID)
        norm_back(
            targets[SECOND_RESID],
            row(GAIN_ROW + 2 * layer + 1),
            GAIN_ROW + 2 * layer + 1,
            6 * layer + 5,
            6 * layer + 4,
        )
        if layer:
            load(SECOND_RESID, layer - 1)
        copies.wait(ACTIVE)
        for panel in range(4):
            grad = dot(targets[ACTIVE][panel], d_low[...], TN)
            out_rows = pl.ds((layer * PANELS + OUT_AT) * PART, 4 * PART)
            deliver(grad, partial.at[panel, :, :, out_rows, :], (2, 2, 4 * PART, D))
            if base and panel == 1:
                run(base - 1)
        if layer:
            load(ACTIVE, layer - 1)
        for panel in range(3, -1, -1):
            slot = panel % 2
            if panel:
                load_hidden(layer, panel - 1)
            else:
                for at in range(4):
                    fetch(at, layer, attention_weights.at[at])
            copies.wait((SLOPE, slot), (WEIGHT, OUT_AT + panel))
            value = dot(d_low[...], matrix(out_weights.at[slot]), NT) * slope[slot].astype(WIDE)
            grads[pl.ds(HIDDEN_ROW + 4 * layer + panel, 1), :] = column_sum(value)
            d_upward[...] = value.astype(LOW)
            pause(base + 2 * (3 - panel) + 1)
            copies.wait(FIRST_LOW, (WEIGHT, IN_AT + panel))
            deliver_panel(dot(targets[FIRST_LOW][...], d_upward[...], TN), layer, IN_AT + panel)
            flow[...] += dot(d_upward[...], matrix(in_weights.at[slot]), NT)
            run(base + 2 * (3 - panel) + 2)
        if layer:
            load_hidden(layer - 1, 3)
            load(FIRST_LOW, layer - 1)
        copies.wait(FIRST_RESID)
        norm_back(
            targets[FIRST_RESID],
            row(GAIN_ROW + 2 * layer),
            GAIN_ROW + 2 * layer,
            6 * layer + 3,
            6 * layer + 2,
        )
        if layer:
            load(FIRST_RESID, layer - 1)
        copies.wait(CONTEXT, (WEIGHT, O_AT))
        deliver_panel(dot(targets[CONTEXT][...], d_low[...], TN), layer, O_AT)
        d_context[...] = dot(d_low[...], matrix(attention_weights.at[O_AT]), NT).astype(LOW)
        pause(base + 9)
        copies.wait(PACKED, EXTENDED)

        def heads(pair, carry):
            attend_back(
                pair,
                targets[PACKED],
                targets[EXTENDED],
                targets[CONTEXT],
                d_context,
                d_packed,
                d_keys,
                d_values,
                spans,
            )
            advance(
                rounds, base + 9 + (2 * pair) // 3, base + 9 + (2 * pair + 2) // 3
            )
            return carry

        lax.fori_loop(0, PAIRS, heads, 0)
        spent[0] = base + 13
        if layer:
            for which in (PACKED, EXTENDED, CONTEXT):
                load(which, layer - 1)
        copies.wait(KEPT_LOW, (WEIGHT, 0), (WEIGHT, 1), (WEIGHT, 2))
        for panel in (V_AT, K_AT, Q_AT):
            deliver_panel(dot(targets[KEPT_LOW][...], d_packed[panel], TN), layer, panel)
            flow[...] += dot(d_packed[panel], matrix(attention_weights.at[panel]), NT)
            if panel != K_AT:
                at = 6 * layer + (0 if panel == Q_AT else 1)
                grads[pl.ds(at, 1), :] = column_sum(d_packed[panel].astype(WIDE))
            pause(base + 14 + (V_AT - panel))
        if layer:
            load(KEPT_LOW, layer - 1)
    d_hidden[...] = flow[...].astype(LOW)
    small[...] = jnp.broadcast_to(grads[...].astype(LOW)[None, None, None], small.shape)
    copies.start(SMALL, small, partial.at[:, :, :, pl.ds(tail, PAIR), :])
    copies.wait_all()
    if near:
        rounds.drain(spent[0])


HELD_BACK = (SECOND_RESID, FIRST_RESID, KEPT_LOW, PACKED, CONTEXT, EXTENDED, FIRST_LOW, ACTIVE)


def backward(qry_grad, psg_grad, qry_len, psg_len, whole, kept, layers, near):
    here, scalars, far = places()
    rows = whole.shape[3]
    outs = [jax.ShapeDtypeStruct(whole.shape, LOW), jax.ShapeDtypeStruct((D, D), LOW)]
    specs = [far, here]
    if near:
        outs.append(jax.ShapeDtypeStruct((rows, D), WIDE))
        specs.append(far)
    panel = (4, 2, 2, PART, D)
    scratch = [pltpu.VMEM(*KEPT[which]) for which in HELD_BACK]
    scratch += [
        vmem(2, D, D),
        vmem(D, D, dtype=WIDE),
        vmem(D, D),
        vmem(D, D),
        vmem(3, D, D),
        vmem(D, D),
        vmem(4, *panel),
        vmem(2, *panel),
        vmem(2, 2, 2, 4 * PART, D),
        vmem(4, D, D),
        vmem(4, 2, 2, PAIR, D),
        vmem(PAIR, D, dtype=WIDE),
        vmem(PAIR, D, dtype=WIDE),
        vmem(LONG, 128, dtype=WIDE),
        vmem(LONG, 128, dtype=WIDE),
        pltpu.SemaphoreType.DMA((32,)),
    ]
    shapes = {}
    if near:
        shapes = scatter_scratch()
        scratch += transfer_scratch()
        scratch += [vmem(DEPTH, *s, dtype=t) for s, t in shapes.values()]
    return pl.pallas_call(
        functools.partial(backward_kernel, near, layers, rows // PAIR, tuple(shapes)),
        out_shape=outs,
        in_specs=[here, here, scalars, scalars, far] + [far] * len(KEPT),
        out_specs=specs,
        scratch_shapes=scratch,
        compiler_params=params_of(1 if near else None),
        name="backward",
    )(qry_grad, psg_grad, qry_len, psg_len, whole, *kept)


def unpack_kernel(layers, part, total, qkv, o, inward, outward, semaphores):
    copies = Pending(semaphores)
    for layer in range(layers):
        base = layer * PANELS
        for ref, panels, first in ((qkv, 3, Q_AT), (o, 1, O_AT), (inward, 4, IN_AT)):
            for panel in range(panels):
                copies.start(
                    (layer, first + panel),
                    total.at[pl.ds((base + first + panel) * part, part), :],
                    ref.at[layer, :, pl.ds(panel * D, D)],
                )
        copies.start(
            (layer, OUT_AT),
            total.at[pl.ds((base + OUT_AT) * part, 4 * part), :],
            outward.at[layer],
        )
    copies.wait_all()


def unpack(total, layers, part):
    here, _scalars, far = places()
    shapes = [(layers, part, 3 * D), (layers, part, D), (layers, part, 4 * D), (layers, 4 * part, D)]
    return pl.pallas_call(
        functools.partial(unpack_kernel, layers, part),
        out_shape=[jax.ShapeDtypeStruct(shape, WIDE) for shape in shapes],
        in_specs=[here],
        out_specs=[far] * 4,
        scratch_shapes=[pltpu.SemaphoreType.DMA((32,))],
        compiler_params=pltpu.CompilerParams(vmem_limit_bytes=VMEM_BYTES),
        name="unpack",
    )(total)


def small_rows(biases, gains, in_bias, at, parts, part):
    rows = [biases.reshape(-1, part), gains.reshape(-1, part)]
    span = D // (4 * part)
    lane = lax.broadcasted_iota(jnp.int32, (1, D), 1)
    small = jnp.concatenate(rows, axis=0)
    small = jnp.where(lane // part == at, jnp.tile(small, (1, parts)), jnp.zeros((), small.dtype))
    placed = jnp.tile(in_bias, (1, span))[:, None, :]
    panel = lax.broadcasted_iota(jnp.int32, (1, 4, 1), 1)
    mine = jnp.logical_and(panel == at // span, (lane // (4 * part) == at % span)[None])
    placed = jnp.where(mine, placed, jnp.zeros((), placed.dtype)).reshape(-1, D)
    small = jnp.concatenate([small, placed], axis=0)
    return jnp.pad(small, ((0, PAIR - small.shape[0]), (0, 0)))


def far_whole(w_qkv, w_o, w_in, w_out, small, layers):
    def gathered(weight, width):
        every = lax.all_gather(weight, "fsdp", axis=1, tiled=True)
        every = every.reshape(layers, D, width, D).transpose(0, 2, 1, 3)
        return every.reshape(layers, width, 16, PART, D)

    outward = lax.all_gather(w_out, "fsdp", axis=1, tiled=True)
    outward = outward.reshape(layers, 16, 4, PART, D).transpose(0, 2, 1, 3, 4)
    parts = [gathered(w_qkv, 3), gathered(w_o, 1), gathered(w_in, 4), outward]
    panels = jnp.concatenate(parts, axis=1).transpose(2, 0, 1, 3, 4).reshape(16, -1, D)
    small = lax.psum(small.astype(WIDE), "fsdp").astype(LOW)
    small = jnp.pad(small[None], ((0, 15), (0, 0), (0, 0)))
    return jnp.concatenate([panels, small], axis=1).reshape(4, 2, 2, -1, D)


def far_total(partial, layers, part):
    partial = partial.reshape(16, -1, D).astype(WIDE)
    panels = layers * PANELS
    grads = partial[:, : panels * PART].reshape(16, layers, PANELS, PART, D)
    inner = grads[:, :, :OUT_AT].transpose(1, 2, 0, 3, 4).reshape(layers, OUT_AT, -1, part, D)
    outer = grads[:, :, OUT_AT:].transpose(1, 0, 2, 3, 4).reshape(layers, -1, 4, part, D)
    both = jnp.concatenate([inner.transpose(2, 0, 1, 3, 4), outer.transpose(1, 0, 2, 3, 4)], axis=2)
    total = lax.psum_scatter(both.reshape(-1, panels * part, D), "fsdp", scatter_dimension=0)
    small = lax.psum(partial[0, panels * PART :], ("rep", "fsdp"))
    return jnp.concatenate([lax.psum(total, "rep"), small], axis=0)


def shards(
    hidden,
    qry_len,
    psg_len,
    qry_grad,
    psg_grad,
    w_qkv,
    w_o,
    w_in,
    w_out,
    biases,
    gains,
    in_bias,
    parts,
    near,
):
    layers, part = w_qkv.shape[0], w_qkv.shape[1]
    at = lax.axis_index("fsdp")
    small = small_rows(biases, gains, in_bias, at, parts, part)
    sources = (w_qkv, w_o, w_in, w_out, small)
    if not near:
        sources = (far_whole(*sources, layers),)
    whole, mixed, kept = forward(hidden, qry_len, psg_len, sources, layers, near)
    found = backward(qry_grad, psg_grad, qry_len, psg_len, whole, kept, layers, near)
    total = found[2] if near else far_total(found[0], layers, part)
    panels = layers * PANELS * part
    if near:
        matrices = unpack(total, layers, part)
    else:
        grads = total[:panels].reshape(layers, PANELS, part, D)
        matrices = [
            grads[:, first:last].transpose(0, 2, 1, 3).reshape(layers, part, -1)
            for first, last in ((Q_AT, O_AT), (O_AT, IN_AT), (IN_AT, OUT_AT))
        ]
        matrices.append(grads[:, OUT_AT:].reshape(layers, 4 * part, D))
    small = lax.dynamic_slice(total, (panels, at * part), (HIDDEN_ROW, part))
    span = D // (4 * part)
    d_in_bias = total[panels + HIDDEN_ROW : panels + SMALL_ROWS].reshape(layers, 4, D)
    d_in_bias = lax.dynamic_slice(
        d_in_bias, (0, at // span, at % span * 4 * part), (layers, 1, 4 * part)
    )
    return (
        mixed,
        found[1],
        *matrices,
        small[:GAIN_ROW].reshape(layers, 6, part),
        small[GAIN_ROW:].reshape(layers, 2, part),
        d_in_bias.reshape(layers, 4 * part),
    )


def solution(mesh):
    both, cut = ("rep", "fsdp"), P(None, "fsdp")
    rows, last = P(both), P(None, None, "fsdp")
    parts = mesh.shape["fsdp"]
    near = parts == 16 and mesh.shape["rep"] == 2
    return jax.shard_map(
        functools.partial(shards, parts=parts, near=near),
        mesh=mesh,
        in_specs=(rows, rows, rows, rows, rows, cut, cut, cut, cut, last, last, cut),
        out_specs=(rows, rows, cut, cut, cut, cut, last, last, cut),
        check_vma=False,
    )
```

```python
import functools

import jax
import jax.numpy as jnp
from jax import lax
from jax.experimental import pallas as pl
from jax.experimental.pallas import tpu as pltpu
from jax.sharding import PartitionSpec as P

MESH = pl.DeviceIdType.MESH
LOW, WIDE = jnp.bfloat16, jnp.float32
D = 768
HALF = 64
SHORT = 128
LONG = 512
PAIRS = D // 128
NORM_EPS = 1e-12
MASKED = -1e30
VMEM_BYTES = 60 * 2**20
NN = (((1,), (0,)), ((), ()))
NT = (((1,), (1,)), ((), ()))
TN = (((0,), (0,)), ((), ()))

BLK = 16
PAIR = 2 * BLK
LAG = 2
DEPTH = 4
X, Y, Z, CORE = 0, 1, 2, 3
SIZES = {X: 2, Y: 2, Z: 4}
ROUTES = (
    ((X, Z, Y), 0, 128),
    ((Y, Z, X), 128, 128),
    ((Z, X, Y), 256, 256),
    ((Z, Y, X), 512, 256),
)
MINE, THEIRS, SUMMED, FINAL, LAND, HELD = range(6)

Q_AT, K_AT, V_AT, O_AT, IN_AT, OUT_AT, PANELS = 0, 1, 2, 3, 4, 8, 12
PART = D // 16
LAYER_CHUNKS = PANELS * PART // PAIR
GAIN_ROW, HIDDEN_ROW, SMALL_ROWS = 12, 16, 24


def steps_of(axis):
    return (1, 2, 3) if axis == Z else (1,)


class Place:
    def __init__(self):
        core = lax.axis_index("rep")
        spot = lax.axis_index("fsdp")
        x, y, z = lax.rem(spot, 2), lax.rem(spot // 2, 2), spot // 4
        self.core = core
        self.at = {X: x, Y: y, Z: z}
        self.to = {
            (CORE, 1): (1 - core, spot),
            (X, 1): (core, spot + 1 - 2 * x),
            (Y, 1): (core, spot + 2 - 4 * y),
        }
        self.next_z = {}
        for step in (1, 2, 3):
            other = lax.rem(z + step, 4)
            self.next_z[step] = other
            self.to[Z, step] = (core, other * 4 + y * 2 + x)

    def greet(self):
        barrier = pltpu.get_barrier_semaphore()
        for device in self.to.values():
            pl.semaphore_signal(barrier, inc=1, device_id=device, device_id_type=MESH)
        pl.semaphore_wait(barrier, len(self.to))


STAGES = 5


def when_in(chunk, count, work):
    pl.when(jnp.logical_and(chunk >= 0, chunk < count))(work)


class Rounds:
    stages = 0

    def __init__(self, place, send, recv, local, count):
        self.place, self.send, self.recv, self.local, self.count = place, send, recv, local, count
        self.rounds = count + self.stages * LAG

    def remote(self, source, target, stage, slot, partner):
        return pltpu.make_async_remote_copy(
            src_ref=source,
            dst_ref=target,
            send_sem=self.send.at[stage, slot],
            recv_sem=self.recv.at[stage, slot],
            device_id=self.place.to[partner],
            device_id_type=MESH,
        )

    def await_all(self, chunk, stage):
        slot = lax.rem(chunk, DEPTH)
        as_large = self.as_large(stage)
        for semaphores in (self.send, self.recv):
            pltpu.make_async_copy(as_large, as_large, semaphores.at[stage, slot]).wait()
        for copy in self.local_copies(chunk, stage):
            copy.wait()

    def rows(self, chunk, core):
        return pl.ds(pl.multiple_of(self.spot(chunk) * PAIR + core * BLK, BLK), BLK)

    def finish(self, number):
        for stage in range(self.stages):
            chunk = number - LAG * stage - LAG

            def work(chunk=chunk, stage=stage):
                self.await_all(chunk, stage)
                self.finished(chunk, stage)

            when_in(chunk, self.count, work)

    def begin(self, number):
        for stage in range(self.stages):
            chunk = number - LAG * stage

            def work(chunk=chunk, stage=stage):
                for copy in self.local_copies(chunk, stage) + self.copies(chunk, stage):
                    copy.start()

            when_in(chunk, self.count, work)

    def round(self, number):
        self.finish(number)
        self.begin(number)

    def drain(self, begin):
        def body(step, carry):
            number = begin + 2 * step
            self.finish(number)
            self.finish(number + 1)
            self.begin(number)
            self.begin(number + 1)
            return carry

        lax.fori_loop(0, (self.rounds - begin + 1) // 2, body, 0)

    def tiles(self, stage):
        count = 0
        for order, _first, width in ROUTES:
            blocks = 1
            for axis in order[:stage]:
                blocks *= SIZES[axis]
            count += blocks * (width // 128) * len(steps_of(order[stage]))
        return count

    def local_copies(self, chunk, stage):
        return []

    def finished(self, chunk, stage):
        pass


class Gather(Rounds):
    stages = 4

    def __init__(self, own, whole, *rest):
        super().__init__(*rest)
        self.own, self.whole = own, whole

    def spot(self, chunk):
        return lax.rem(chunk + self.count - 1, self.count)

    def copies(self, chunk, stage):
        at = self.place.at
        slot = lax.rem(chunk, DEPTH)
        rows = self.rows(chunk, self.place.core)
        if stage == 3:
            part = self.whole.at[:, :, :, rows, :]
            return [self.remote(part, part, stage, slot, (CORE, 1))]
        found = []
        for route, (order, first, width) in enumerate(ROUTES):
            axis, done = order[stage], order[:stage]
            columns = pl.ds(first, width)
            if stage == 0:
                source = self.own.at[rows, columns]
                part = self.whole.at[at[Z], at[Y], at[X], rows, columns]
            else:
                spans = [
                    pl.ds(0, SIZES[name]) if name in done else pl.ds(at[name], 1)
                    for name in (Z, Y, X)
                ]
                source = part = self.whole.at[spans[0], spans[1], spans[2], rows, columns]
            for step in steps_of(axis):
                found.append(self.remote(source, part, stage, slot, (axis, step)))
        return found

    def as_large(self, stage):
        if stage == 3:
            return self.whole.at[:, :, :, pl.ds(0, BLK), :]
        return self.whole.at[0, 0, 0, pl.ds(0, BLK * self.tiles(stage)), pl.ds(0, 128)]

    def local_copies(self, chunk, stage):
        if stage:
            return []
        at = self.place.at
        rows = self.rows(chunk, self.place.core)
        return [
            pltpu.make_async_copy(
                self.own.at[rows, :],
                self.whole.at[at[Z], at[Y], at[X], rows, :],
                self.local.at[0, lax.rem(chunk, DEPTH)],
            )
        ]


class Scatter(Rounds):
    stages = 5

    def __init__(self, partial, total, work, *rest):
        super().__init__(*rest)
        self.partial, self.total, self.work = partial, total, work

    def spot(self, chunk):
        return lax.rem(2 * self.count - 2 - chunk, self.count)

    def copies(self, chunk, stage):
        core, at = self.place.core, self.place.at
        slot = lax.rem(chunk, DEPTH)
        rows = self.rows(chunk, core)
        if stage == 0:
            theirs = self.partial.at[:, :, :, self.rows(chunk, 1 - core), :]
            landing = self.work[THEIRS].at[slot]
            return [self.remote(theirs, landing, stage, slot, (CORE, 1))]
        if stage == 4:
            source, target = self.work[FINAL].at[slot], self.total.at[rows, :]
            return [self.remote(source, target, stage, slot, (CORE, 1))]
        found = []
        for route, (gather_order, first, width) in enumerate(ROUTES):
            order = gather_order[::-1]
            axis, left = order[stage - 1], [n for n in (Z, Y, X) if n not in order[: stage - 1]]
            if stage == 1:
                held, columns = self.work[SUMMED].at[slot], pl.ds(first, width)
            else:
                held, columns = self.work[HELD, route, stage - 1].at[slot], slice(None)
            landing = self.work[LAND, route, stage].at[slot]
            for step in steps_of(axis):
                to = self.place.next_z[step] if axis == Z else 1 - at[axis]
                index = tuple(to if name == axis else slice(None) for name in left)
                found.append(
                    self.remote(
                        held.at[index + (slice(None), columns)],
                        landing.at[step - 1] if axis == Z else landing,
                        stage,
                        slot,
                        (axis, step),
                    )
                )
        return found

    def as_large(self, stage):
        if stage == 0:
            return self.work[THEIRS].at[0]
        if stage == 4:
            return self.work[FINAL].at[0]
        return self.partial.at[0, 0, 0, pl.ds(0, BLK * self.tiles(3 - stage)), pl.ds(0, 128)]

    def local_copies(self, chunk, stage):
        slot = lax.rem(chunk, DEPTH)
        rows = self.rows(chunk, self.place.core)
        if stage == 0:
            mine = self.partial.at[:, :, :, rows, :]
            return [pltpu.make_async_copy(mine, self.work[MINE].at[slot], self.local.at[0, slot])]
        if stage == 4:
            final = self.work[FINAL].at[slot]
            return [pltpu.make_async_copy(final, self.total.at[rows, :], self.local.at[1, slot])]
        return []

    def finished(self, chunk, stage):
        at = self.place.at
        slot = lax.rem(chunk, DEPTH)
        if stage == 0:
            self.work[SUMMED][slot] = self.work[MINE][slot] + self.work[THEIRS][slot]
        if stage in (0, 4):
            return
        for route, (gather_order, first, width) in enumerate(ROUTES):
            order = gather_order[::-1]
            axis, left = order[stage - 1], [n for n in (Z, Y, X) if n not in order[: stage - 1]]
            if stage == 1:
                held, columns = self.work[SUMMED], slice(first, first + width)
            else:
                held, columns = self.work[HELD, route, stage - 1], slice(None)
            index = tuple(at[axis] if name == axis else slice(None) for name in left)
            value = held[(slot,) + index + (slice(None), columns)]
            landing = self.work[LAND, route, stage]
            if axis == Z:
                value = value.astype(WIDE)
                for step in (1, 2, 3):
                    value = value + landing[slot, step - 1].astype(WIDE)
            elif stage == 3:
                value = value.astype(WIDE) + landing[slot].astype(WIDE)
            else:
                value = value + landing[slot]
            if stage == 3:
                self.work[FINAL][slot, :, first : first + width] = value
            else:
                self.work[HELD, route, stage][slot] = value.astype(LOW)


def scatter_scratch():
    shapes = {
        MINE: ((4, 2, 2, BLK, D), LOW),
        THEIRS: ((4, 2, 2, BLK, D), LOW),
        SUMMED: ((4, 2, 2, BLK, D), LOW),
        FINAL: ((BLK, D), WIDE),
    }
    for route, (gather_order, first, width) in enumerate(ROUTES):
        order = gather_order[::-1]
        for stage in (1, 2, 3):
            left = tuple(SIZES[n] for n in (Z, Y, X) if n not in order[:stage])
            steps = (3,) if order[stage - 1] == Z else ()
            shapes[LAND, route, stage] = (steps + left + (BLK, width), LOW)
            if stage < 3:
                shapes[HELD, route, stage] = (left + (BLK, width), LOW)
    return shapes


def advance(rounds, begin, end):
    if rounds is None:
        return

    def body(number, carry):
        rounds.round(number)
        return carry

    lax.fori_loop(begin, end, body, 0)


class Pending:
    def __init__(self, semaphores):
        self.semaphores, self.known, self.flying = semaphores, {}, {}

    def start(self, key, source, target):
        self.wait(key)
        at = self.known.setdefault(key, len(self.known))
        copy = pltpu.make_async_copy(source, target, self.semaphores.at[at])
        copy.start()
        self.flying[key] = copy

    def wait(self, *keys):
        for key in keys:
            copy = self.flying.pop(key, None)
            if copy is not None:
                copy.wait()

    def wait_all(self):
        self.wait(*list(self.flying))


def dot(left, right, numbers):
    return lax.dot_general(left, right, numbers, preferred_element_type=WIDE)


def norm_parts(resid):
    average = jnp.mean(resid, axis=-1, keepdims=True)
    centered = resid - average
    spread = jnp.mean(centered * centered, axis=-1, keepdims=True)
    scale = lax.rsqrt(spread + NORM_EPS)
    return centered * scale, scale


def column_sum(value):
    return jnp.sum(value, axis=0, keepdims=True)


def lanes_of(pair):
    return pl.ds(pl.multiple_of(pair * 128, 128), 128)


def sequences(qry_len, psg_len):
    return (
        (2 * SHORT, LONG, psg_len[0]),
        (0, SHORT, qry_len[0]),
        (SHORT, SHORT, qry_len[1]),
    )


def rows_in(size, work):
    def body(step, carry):
        work(pl.ds(pl.multiple_of(step * size, size), size))
        return carry

    lax.fori_loop(0, D // size, body, 0)


def section(ref, layer, first, panels):
    return ref.at[:, :, :, pl.ds((layer * PANELS + first) * PART, panels * PART), :]


def matrix(ref):
    return ref[...].reshape(-1, D)


def place_lanes(shape):
    lane = lax.broadcasted_iota(jnp.int32, shape, 1)
    return lane // HALF, lane % HALF


def dead_rows(length, live):
    row = lax.broadcasted_iota(jnp.int32, (length, 128), 0)
    return jnp.where(row < live, 0.0, MASKED).astype(LOW)


def three_parts(value):
    high = value.astype(LOW)
    rest = value - high.astype(WIDE)
    middle = rest.astype(LOW)
    return high, middle, (rest - middle.astype(WIDE)).astype(LOW)


def attend(pair, packed, context, probs, spans):
    lanes = lanes_of(pair)
    for at, (first, length, live) in enumerate(spans):
        head, lane = place_lanes((length, 128))
        queries = packed[0, first : first + length, lanes] * jnp.array(HALF**-0.5, LOW)
        keys = packed[1, first : first + length, lanes]
        values = packed[2, first : first + length, lanes]
        dead = jnp.where(lane == 0, dead_rows(length, live), jnp.zeros((), LOW))
        unit = jnp.where(lane == 0, 1.0, 0.0).astype(LOW)
        blank = jnp.zeros_like(keys)
        both_probs, both_values = [], []
        for which in range(2):
            scores = dot(
                jnp.where(head == which, keys, dead), jnp.where(head == which, queries, unit), NT
            )
            raised = jnp.exp(scores - jnp.max(scores, axis=0, keepdims=True))
            now = (raised * (1.0 / jnp.sum(raised, axis=0, keepdims=True))).astype(LOW)
            probs[at][which] = now
            both_probs.append(now)
            both_values.append(jnp.where(head == which, values, blank))
        context[first : first + length, lanes] = dot(
            jnp.concatenate(both_probs, axis=0), jnp.concatenate(both_values, axis=0), TN
        ).astype(LOW)


def attend_back(pair, packed, context, probs, d_context, d_packed, spans):
    lanes = lanes_of(pair)
    for at, (first, length, live) in enumerate(spans):
        head, lane = place_lanes((length, 128))
        queries = packed[0, first : first + length, lanes] * jnp.array(HALF**-0.5, LOW)
        keys = packed[1, first : first + length, lanes]
        values = packed[2, first : first + length, lanes]
        upstream = d_context[first : first + length, lanes]
        product = upstream.astype(WIDE) * context[first : first + length, lanes].astype(WIDE)
        ones = jnp.where(lane < 3, 1.0, 0.0).astype(LOW)
        blank = jnp.zeros_like(keys)
        all_probs, all_scores, all_queries, all_keys, all_upstream = [], [], [], [], []
        for which in range(2):
            mine = jnp.where(head == which, upstream, blank)
            all_queries.append(jnp.where(head == which, queries, blank))
            all_keys.append(jnp.where(head == which, keys, blank))
            all_upstream.append(mine)
            inner = jnp.sum(jnp.where(head == which, product, 0.0), axis=1, keepdims=True)
            parts = three_parts(jnp.broadcast_to(-inner, (length, 128)))
            for place, value in enumerate(parts):
                mine = jnp.where(jnp.logical_and(head != which, lane == place), value, mine)
            now = probs[at][which]
            d_probs = dot(jnp.where(head == which, values, ones), mine, NT)
            all_probs.append(now)
            all_scores.append((now.astype(WIDE) * d_probs).astype(LOW))
        d_packed[first : first + length, lanes_of(pair)] = (
            dot(jnp.concatenate(all_scores, axis=0), jnp.concatenate(all_keys, axis=0), TN)
            * (HALF**-0.5)
        ).astype(LOW)
        d_packed[first : first + length, lanes_of(PAIRS + pair)] = dot(
            jnp.concatenate(all_scores, axis=1), jnp.concatenate(all_queries, axis=0), NN
        ).astype(LOW)
        d_packed[first : first + length, lanes_of(2 * PAIRS + pair)] = dot(
            jnp.concatenate(all_probs, axis=1), jnp.concatenate(all_upstream, axis=0), NN
        ).astype(LOW)


KEPT_LOW, PACKED, CONTEXT, FIRST_LOW, ACTIVE, SLOPE, FIRST_RESID, SECOND_RESID, LONG_PROBS, SHORT_PROBS = (
    range(10)
)
KEPT = (
    ((D, D), LOW),
    ((3, D, D), LOW),
    ((D, D), LOW),
    ((D, D), LOW),
    ((4, D, D), LOW),
    ((4, D, D), LOW),
    ((D, D), WIDE),
    ((D, D), WIDE),
    ((PAIRS, 2, LONG, LONG), LOW),
    ((PAIRS, 4, SHORT, SHORT), LOW),
)
WEIGHT, READY, SMALL, OWN = 10, 11, 12, 13


def probs_scratch():
    return [
        vmem(2, 2, LONG, LONG),
        vmem(2, 4, SHORT, SHORT),
        pltpu.SemaphoreType.DMA((2, 2)),
    ]


class Probs:
    def __init__(self, kept, long, short, semaphores):
        self.kept = kept[LONG_PROBS], kept[SHORT_PROBS]
        self.held, self.semaphores = (long, short), semaphores

    def of(self, pair):
        slot = lax.rem(pair, 2)
        long, short = (ref.at[slot] for ref in self.held)
        return long, short.at[pl.ds(0, 2)], short.at[pl.ds(2, 2)]

    def copies(self, layer, pair, save):
        slot = lax.rem(pair, 2)
        found = []
        for which in range(2):
            here, there = self.held[which].at[slot], self.kept[which].at[layer, pair]
            source, target = (here, there) if save else (there, here)
            found.append(pltpu.make_async_copy(source, target, self.semaphores.at[which, slot]))
        return found

    def start(self, layer, pair, save):
        for copy in self.copies(layer, pair, save):
            copy.start()

    def wait(self, layer, pair, save):
        for copy in self.copies(layer, pair, save):
            copy.wait()


def forward_kernel(near, layers, count, *refs):
    hidden, qry_len, psg_len = refs[:3]
    if near:
        w_qkv, w_o, w_in, w_out, small_own, whole = refs[3:9]
        refs = refs[9:]
    else:
        whole, refs = refs[3], refs[4:]
    mixed, kept, refs = refs[0], refs[1 : 1 + len(KEPT)], refs[1 + len(KEPT) :]
    (state, total, resid, low, packed, context, first_low, active, slope) = refs[:9]
    (attention_weights, in_weights, out_weights, small, params, semaphores) = refs[9:15]
    probs, refs = Probs(kept, *refs[15:18]), refs[18:]
    rounds = None
    copies = Pending(semaphores)
    if near:
        place, own = Place(), refs[0]
        for layer in range(layers):
            base = layer * PANELS
            blocks = [(w_qkv, 3, Q_AT), (w_o, 1, O_AT), (w_in, 4, IN_AT)]
            for ref, panels, first in blocks:
                for panel in range(panels):
                    copies.start(
                        (OWN, layer, first + panel),
                        ref.at[layer, :, pl.ds(panel * D, D)],
                        own.at[pl.ds((base + first + panel) * PART, PART), :],
                    )
            copies.start(
                (OWN, layer, OUT_AT),
                w_out.at[layer],
                own.at[pl.ds((base + OUT_AT) * PART, 4 * PART), :],
            )
        copies.start((OWN, layers, 0), small_own, own.at[pl.ds(layers * PANELS * PART, PAIR), :])
        place.greet()
        copies.wait_all()
        rounds = Gather(own, whole, place, *refs[1:4], count)
    spans = sequences(qry_len, psg_len)

    def keep(which, layer, ref, panel=None):
        target = kept[which].at[layer] if panel is None else kept[which].at[layer, panel]
        copies.start((which, panel), ref, target)

    def fetch(panel, layer, target):
        copies.start((WEIGHT, panel), section(whole, layer, panel, 1), target)

    spent = [0]

    def run(end):
        if near:
            end = min(end, rounds.rounds)
        if end > spent[0]:
            advance(rounds, spent[0], end)
            spent[0] = end

    run(9)
    copies.start(SMALL, whole.at[:, :, :, pl.ds(layers * PANELS * PART, PAIR), :], small)
    state[...] = hidden[...].astype(WIDE)
    low[...] = hidden[...]
    keep(KEPT_LOW, 0, low)
    copies.wait(SMALL)
    params[...] = jnp.sum(small[...].astype(WIDE), axis=(0, 1, 2))

    def row(at):
        return params[pl.ds(at, 1), :]

    run(14)
    for panel in (Q_AT, K_AT, V_AT):
        fetch(panel, 0, attention_weights.at[panel])
    for layer in range(layers):
        base = LAYER_CHUNKS * layer
        copies.wait((PACKED, None))
        for panel in (Q_AT, K_AT, V_AT):
            copies.wait((WEIGHT, panel))
            value = dot(low[...], matrix(attention_weights.at[panel]), NN)
            if panel != K_AT:
                value = value + row(6 * layer + (0 if panel == Q_AT else 1))
            packed[panel] = value.astype(LOW)
            run(base + 15 + panel)
        keep(PACKED, layer, packed)
        fetch(O_AT, layer, attention_weights.at[O_AT])
        fetch(IN_AT, layer, in_weights.at[0])
        copies.wait((CONTEXT, None))

        def heads(pair, carry):
            if layer:
                probs.wait(layer, pair, True)
            else:
                pl.when(pair >= 2)(lambda: probs.wait(layer, pair, True))
            attend(pair, packed, context, probs.of(pair), spans)
            probs.start(layer, pair, True)
            advance(rounds, base + 17 + pair // 2, base + 17 + (pair + 1) // 2)
            return carry

        lax.fori_loop(0, PAIRS, heads, 0)
        spent[0] = base + 20
        keep(CONTEXT, layer, context)
        fetch(IN_AT + 1, layer, in_weights.at[1])
        copies.wait((WEIGHT, O_AT), (SECOND_RESID, None))
        total[...] = dot(context[...], matrix(attention_weights.at[O_AT]), NN)
        run(base + 21)
        copies.wait((FIRST_RESID, None), (FIRST_LOW, None))

        def normalise_first(rows):
            value = state[rows, :] + (total[rows, :] + row(6 * layer + 2))
            resid[rows, :] = value
            norm = norm_parts(value)[0] * row(GAIN_ROW + 2 * layer) + row(6 * layer + 3)
            first_low[rows, :] = norm.astype(LOW)
            total[rows, :] = norm + row(6 * layer + 4)

        rows_in(128, normalise_first)
        keep(FIRST_RESID, layer, resid)
        keep(FIRST_LOW, layer, first_low)
        for panel in range(4):
            copies.wait((WEIGHT, IN_AT + panel))
            copies.wait((ACTIVE, panel), (SLOPE, panel), (SLOPE, (panel + 2) % 4))

            def inward(rows):
                upward = dot(first_low[rows, :], matrix(in_weights.at[panel % 2]), NN)
                upward = upward + row(HIDDEN_ROW + 4 * layer + panel)
                share = 0.5 + 0.5 * lax.erf(upward * (0.5**0.5))
                bell = jnp.exp(upward * upward * -0.5) * 0.3989422804014327
                active[panel, rows, :] = (upward * share).astype(LOW)
                slope[panel % 2, rows, :] = (share + upward * bell).astype(LOW)

            rows_in(384, inward)
            keep(ACTIVE, layer, active.at[panel], panel)
            keep(SLOPE, layer, slope.at[panel % 2], panel)
            if panel < 2:
                fetch(IN_AT + panel + 2, layer, in_weights.at[panel])
            run(base + 22 + panel)
        run(base + 27)
        for panel in range(4):
            rows = pl.ds((layer * PANELS + OUT_AT) * PART, 4 * PART)
            copies.start(
                (WEIGHT, OUT_AT + panel), whole.at[panel, :, :, rows, :], out_weights.at[panel]
            )
        for panel in range(4):
            copies.wait((WEIGHT, OUT_AT + panel))
            total[...] += dot(active[panel], matrix(out_weights.at[panel]), NN)
            if layer + 1 < layers and panel % 2:
                run(base + 28 + panel // 2)
        if layer + 1 < layers:
            run(base + 32)
            for panel in (Q_AT, K_AT, V_AT):
                fetch(panel, layer + 1, attention_weights.at[panel])
        copies.wait((KEPT_LOW, None))

        def normalise_second(rows):
            norm = norm_parts(total[rows, :])[0]
            value = norm * row(GAIN_ROW + 2 * layer + 1) + row(6 * layer + 5)
            state[rows, :] = value
            low[rows, :] = value.astype(LOW)

        keep(SECOND_RESID, layer, total)
        rows_in(128, normalise_second)
        if layer == layers - 1:
            mixed[...] = low[...]
        else:
            keep(KEPT_LOW, layer + 1, low)
    for pair in (PAIRS - 2, PAIRS - 1):
        probs.wait(layers - 1, pair, True)
    copies.wait_all()


def vmem(*shape, dtype=LOW):
    return pltpu.VMEM(shape, dtype)


def places():
    return (
        pl.BlockSpec(memory_space=pltpu.VMEM),
        pl.BlockSpec(memory_space=pltpu.SMEM),
        pl.BlockSpec(memory_space=pl.ANY),
    )


def transfer_scratch():
    return [
        pltpu.SemaphoreType.DMA((STAGES, DEPTH)),
        pltpu.SemaphoreType.DMA((STAGES, DEPTH)),
        pltpu.SemaphoreType.DMA((2, DEPTH)),
    ]


def params_of(identity):
    extra = {}
    if identity is not None:
        extra = dict(collective_id=identity, has_side_effects=True)
    return pltpu.CompilerParams(vmem_limit_bytes=VMEM_BYTES, **extra)


def forward(hidden, qry_len, psg_len, sources, layers, near):
    here, scalars, far = places()
    rows = layers * PANELS * PART + PAIR
    outs = [jax.ShapeDtypeStruct((D, D), LOW)]
    outs += [jax.ShapeDtypeStruct((layers,) + s, t) for s, t in KEPT]
    specs = [here] + [far] * len(KEPT)
    if near:
        outs = [jax.ShapeDtypeStruct((4, 2, 2, rows, D), LOW)] + outs
        specs = [far] + specs
    panel = (4, 2, 2, PART, D)
    scratch = [
        vmem(D, D, dtype=WIDE),
        vmem(D, D, dtype=WIDE),
        vmem(D, D, dtype=WIDE),
        vmem(D, D),
        vmem(3, D, D),
        vmem(D, D),
        vmem(D, D),
        vmem(4, D, D),
        vmem(2, D, D),
        vmem(4, *panel),
        vmem(2, *panel),
        vmem(4, 2, 2, 4 * PART, D),
        vmem(4, 2, 2, PAIR, D),
        vmem(PAIR, D, dtype=WIDE),
        pltpu.SemaphoreType.DMA((64,)),
    ] + probs_scratch()
    if near:
        scratch += [vmem(rows, D)] + transfer_scratch()
    found = pl.pallas_call(
        functools.partial(forward_kernel, near, layers, rows // PAIR),
        out_shape=outs,
        in_specs=[here, scalars, scalars] + [far] * len(sources),
        out_specs=specs,
        scratch_shapes=scratch,
        compiler_params=params_of(0 if near else None),
        name="forward",
    )(hidden, qry_len, psg_len, *sources)
    if near:
        return found[0], found[1], found[2:]
    return sources[0], found[0], found[1:]


def backward_kernel(near, layers, count, names, *refs):
    qry_grad, psg_grad, qry_len, psg_len, whole = refs[:5]
    kept, refs = refs[5 : 5 + len(KEPT)], refs[5 + len(KEPT) :]
    partial, d_hidden, refs = refs[0], refs[1], refs[2:]
    if near:
        sums, refs = refs[0], refs[1:]
    targets, refs = dict(zip(HELD_BACK, refs)), refs[len(HELD_BACK) :]
    (slope, flow, d_low, d_context, d_packed, d_upward, attention_weights, in_weights) = refs[:8]
    (out_weights, ready, small, params, grads, semaphores) = refs[8:14]
    probs, refs = Probs(kept, *refs[14:17]), refs[17:]
    rounds = None
    if near:
        place = Place()
        place.greet()
        work = dict(zip(names, refs[3:]))
        rounds = Scatter(partial, sums, work, place, *refs[:3], count)
    copies = Pending(semaphores)
    spans = sequences(qry_len, psg_len)
    tail = layers * PANELS * PART

    def load(which, layer):
        copies.start(which, kept[which].at[layer], targets[which])

    def fetch(panel, layer, target):
        copies.start((WEIGHT, panel), section(whole, layer, panel, 1), target)

    def fetch_out(layer, panel):
        rows = pl.ds((layer * PANELS + OUT_AT) * PART, 4 * PART)
        copies.start(
            (WEIGHT, OUT_AT + panel), whole.at[panel, :, :, rows, :], out_weights.at[panel % 2]
        )

    def load_hidden(layer, panel):
        copies.start((SLOPE, panel % 2), kept[SLOPE].at[layer, panel], slope.at[panel % 2])
        fetch_out(layer, panel)
        fetch(IN_AT + panel, layer, in_weights.at[panel % 2])

    turn = [0]

    def deliver(value, target, shape):
        at = turn[0] % 4
        turn[0] += 1
        copies.wait((READY, at))
        ready[at] = value.astype(LOW)
        copies.start((READY, at), ready.at[at].reshape(shape), target)

    def pause(end, newest=0):
        copies.wait(*[(READY, (turn[0] + at) % 4) for at in range(4 - newest)])
        run(end)

    def deliver_panel(value, layer, panel):
        deliver(value, section(partial, layer, panel, 1), (4, 2, 2, PART, D))

    def row(at):
        return params[pl.ds(at, 1), :]

    copies.start(SMALL, whole.at[:, :, :, pl.ds(tail, PAIR), :], small)
    for which in (SECOND_RESID, ACTIVE):
        load(which, layers - 1)
    load_hidden(layers - 1, 3)
    for which in (FIRST_LOW, FIRST_RESID, CONTEXT, PACKED, KEPT_LOW):
        load(which, layers - 1)
    probs.start(layers - 1, 0, False)
    grads[...] = jnp.zeros_like(grads)
    for at, (first, length, live) in enumerate(spans):
        upstream = psg_grad[...] if at == 0 else qry_grad[at - 1 : at, :]
        alive = lax.broadcasted_iota(jnp.int32, (length, D), 0) < live
        flow[first : first + length, :] = jnp.where(alive, upstream, 0.0) / live.astype(WIDE)
    copies.wait(SMALL)
    params[...] = jnp.sum(small[...].astype(WIDE), axis=(0, 1, 2))

    def norm_back(resid, gain, gain_row, shift_row, sum_row):
        def block(rows):
            norm, scale = norm_parts(resid[rows, :])
            upstream = flow[rows, :]
            grads[pl.ds(gain_row, 1), :] += column_sum(upstream * norm)
            grads[pl.ds(shift_row, 1), :] += column_sum(upstream)
            scaled = upstream * gain
            result = (
                scaled
                - jnp.mean(scaled, axis=-1, keepdims=True)
                - norm * jnp.mean(scaled * norm, axis=-1, keepdims=True)
            ) * scale
            grads[pl.ds(sum_row, 1), :] += column_sum(result)
            flow[rows, :] = result
            d_low[rows, :] = result.astype(LOW)

        rows_in(128, block)

    spent = [0]

    def run(end):
        if end > spent[0]:
            advance(rounds, spent[0], end)
            spent[0] = end

    for layer in range(layers - 1, -1, -1):
        base = LAYER_CHUNKS * (layers - 1 - layer)
        copies.wait(SECOND_RESID)
        norm_back(
            targets[SECOND_RESID],
            row(GAIN_ROW + 2 * layer + 1),
            GAIN_ROW + 2 * layer + 1,
            6 * layer + 5,
            6 * layer + 4,
        )
        if layer:
            load(SECOND_RESID, layer - 1)
        copies.wait(ACTIVE)
        for panel in range(4):
            grad = dot(targets[ACTIVE][panel], d_low[...], TN)
            out_rows = pl.ds((layer * PANELS + OUT_AT) * PART, 4 * PART)
            deliver(grad, partial.at[panel, :, :, out_rows, :], (2, 2, 4 * PART, D))
            if base and panel == 1:
                run(base)
        if layer:
            load(ACTIVE, layer - 1)
        for panel in range(3, -1, -1):
            slot = panel % 2
            if panel:
                load_hidden(layer, panel - 1)
            else:
                for at in range(4):
                    fetch(at, layer, attention_weights.at[:, :, :, :, pl.ds(at * D, D)])
            copies.wait((SLOPE, slot), (WEIGHT, OUT_AT + panel))
            value = dot(d_low[...], matrix(out_weights.at[slot]), NT) * slope[slot].astype(WIDE)
            grads[pl.ds(HIDDEN_ROW + 4 * layer + panel, 1), :] = column_sum(value)
            d_upward[...] = value.astype(LOW)
            pause(base + 2 * (3 - panel) + 1)
            copies.wait(FIRST_LOW, (WEIGHT, IN_AT + panel))
            deliver_panel(dot(targets[FIRST_LOW][...], d_upward[...], TN), layer, IN_AT + panel)
            flow[...] += dot(d_upward[...], matrix(in_weights.at[slot]), NT)
            run(base + 2 * (3 - panel) + 2)
        if layer:
            load_hidden(layer - 1, 3)
            load(FIRST_LOW, layer - 1)
        copies.wait(FIRST_RESID)
        norm_back(
            targets[FIRST_RESID],
            row(GAIN_ROW + 2 * layer),
            GAIN_ROW + 2 * layer,
            6 * layer + 3,
            6 * layer + 2,
        )
        if layer:
            load(FIRST_RESID, layer - 1)
        copies.wait(CONTEXT, (WEIGHT, O_AT))
        deliver_panel(dot(targets[CONTEXT][...], d_low[...], TN), layer, O_AT)
        out = attention_weights[:, :, :, :, O_AT * D :].reshape(D, D)
        d_context[...] = dot(d_low[...], out, NT).astype(LOW)
        pause(base + 9)
        copies.wait(PACKED)

        def heads(pair, carry):
            pl.when(pair + 1 < PAIRS)(lambda: probs.start(layer, pair + 1, False))
            probs.wait(layer, pair, False)
            attend_back(
                pair,
                targets[PACKED],
                targets[CONTEXT],
                probs.of(pair),
                d_context,
                d_packed,
                spans,
            )
            advance(
                rounds, base + 9 + (2 * pair) // 3, base + 9 + (2 * pair + 2) // 3
            )
            return carry

        lax.fori_loop(0, PAIRS, heads, 0)
        spent[0] = base + 13
        if layer:
            for which in (PACKED, CONTEXT):
                load(which, layer - 1)
            probs.start(layer - 1, 0, False)
        copies.wait(KEPT_LOW, (WEIGHT, 0), (WEIGHT, 1), (WEIGHT, 2))
        for panel in (V_AT, K_AT, Q_AT):
            d_panel = d_packed[:, panel * D : (panel + 1) * D]
            deliver_panel(dot(targets[KEPT_LOW][...], d_panel, TN), layer, panel)
            if panel != K_AT:
                at = 6 * layer + (0 if panel == Q_AT else 1)
                grads[pl.ds(at, 1), :] = column_sum(d_panel.astype(WIDE))
            if panel != V_AT:
                pause(base + 15 + (K_AT - panel), newest=1)
        inward = attention_weights[:, :, :, :, : O_AT * D].reshape(D, O_AT * D)
        flow[...] += dot(d_packed[...], inward, NT)
        pause(base + 17)
        if layer:
            load(KEPT_LOW, layer - 1)
    d_hidden[...] = flow[...].astype(LOW)
    small[...] = jnp.broadcast_to(grads[...].astype(LOW)[None, None, None], small.shape)
    copies.start(SMALL, small, partial.at[:, :, :, pl.ds(tail, PAIR), :])
    copies.wait_all()
    if near:
        rounds.drain(spent[0])


HELD_BACK = (SECOND_RESID, FIRST_RESID, KEPT_LOW, PACKED, CONTEXT, FIRST_LOW, ACTIVE)


def backward(qry_grad, psg_grad, qry_len, psg_len, whole, kept, layers, near):
    here, scalars, far = places()
    rows = whole.shape[3]
    outs = [jax.ShapeDtypeStruct(whole.shape, LOW), jax.ShapeDtypeStruct((D, D), LOW)]
    specs = [far, here]
    if near:
        outs.append(jax.ShapeDtypeStruct((rows, D), WIDE))
        specs.append(far)
    panel = (4, 2, 2, PART, D)
    scratch = [pltpu.VMEM(*KEPT[which]) for which in HELD_BACK]
    scratch += [
        vmem(2, D, D),
        vmem(D, D, dtype=WIDE),
        vmem(D, D),
        vmem(D, D),
        vmem(D, 3 * D),
        vmem(D, D),
        vmem(4, 2, 2, PART, 4 * D),
        vmem(2, *panel),
        vmem(2, 2, 2, 4 * PART, D),
        vmem(4, D, D),
        vmem(4, 2, 2, PAIR, D),
        vmem(PAIR, D, dtype=WIDE),
        vmem(PAIR, D, dtype=WIDE),
        pltpu.SemaphoreType.DMA((32,)),
    ] + probs_scratch()
    shapes = {}
    if near:
        shapes = scatter_scratch()
        scratch += transfer_scratch()
        scratch += [vmem(DEPTH, *s, dtype=t) for s, t in shapes.values()]
    return pl.pallas_call(
        functools.partial(backward_kernel, near, layers, rows // PAIR, tuple(shapes)),
        out_shape=outs,
        in_specs=[here, here, scalars, scalars, far] + [far] * len(KEPT),
        out_specs=specs,
        scratch_shapes=scratch,
        compiler_params=params_of(1 if near else None),
        name="backward",
    )(qry_grad, psg_grad, qry_len, psg_len, whole, *kept)


def unpack_kernel(layers, part, total, qkv, o, inward, outward, biases, gains, in_bias, semaphores):
    copies = Pending(semaphores)
    for layer in range(layers):
        base = layer * PANELS
        for ref, panels, first in ((qkv, 3, Q_AT), (o, 1, O_AT), (inward, 4, IN_AT)):
            for panel in range(panels):
                copies.start(
                    (layer, first + panel),
                    total.at[pl.ds((base + first + panel) * part, part), :],
                    ref.at[layer, :, pl.ds(panel * D, D)],
                )
        copies.start(
            (layer, OUT_AT),
            total.at[pl.ds((base + OUT_AT) * part, 4 * part), :],
            outward.at[layer],
        )
    at, span, tail = lax.axis_index("fsdp"), D // (4 * part), layers * PANELS * part
    mine = pltpu.roll(total[tail : tail + HIDDEN_ROW, :], D - at * part, axis=1)[:, :part]
    for layer in range(layers):
        biases[layer] = mine[6 * layer : 6 * layer + 6]
        gains[layer] = mine[GAIN_ROW + 2 * layer : GAIN_ROW + 2 * layer + 2]
        row = total[pl.ds(tail + HIDDEN_ROW + 4 * layer + at // span, 1), :]
        row = jnp.broadcast_to(row, (8, D))
        row = pltpu.roll(row, D - lax.rem(at, span) * (4 * part), axis=1)
        in_bias[layer : layer + 1, :] = row[:1, : 4 * part]
    copies.wait_all()


def unpack(total, layers, part):
    here, _scalars, far = places()
    shapes = [(layers, part, 3 * D), (layers, part, D), (layers, part, 4 * D), (layers, 4 * part, D)]
    shapes += [(layers, 6, part), (layers, 2, part), (layers, 4 * part)]
    return pl.pallas_call(
        functools.partial(unpack_kernel, layers, part),
        out_shape=[jax.ShapeDtypeStruct(shape, WIDE) for shape in shapes],
        in_specs=[here],
        out_specs=[far] * 4 + [here] * 3,
        scratch_shapes=[pltpu.SemaphoreType.DMA((32,))],
        compiler_params=pltpu.CompilerParams(vmem_limit_bytes=VMEM_BYTES),
        name="unpack",
    )(total)


def small_rows(biases, gains, in_bias, at, parts, part):
    rows = [biases.reshape(-1, part), gains.reshape(-1, part)]
    span = D // (4 * part)
    lane = lax.broadcasted_iota(jnp.int32, (1, D), 1)
    small = jnp.concatenate(rows, axis=0)
    small = jnp.where(lane // part == at, jnp.tile(small, (1, parts)), jnp.zeros((), small.dtype))
    placed = jnp.tile(in_bias, (1, span))[:, None, :]
    panel = lax.broadcasted_iota(jnp.int32, (1, 4, 1), 1)
    mine = jnp.logical_and(panel == at // span, (lane // (4 * part) == at % span)[None])
    placed = jnp.where(mine, placed, jnp.zeros((), placed.dtype)).reshape(-1, D)
    small = jnp.concatenate([small, placed], axis=0)
    return jnp.pad(small, ((0, PAIR - small.shape[0]), (0, 0)))


def far_whole(w_qkv, w_o, w_in, w_out, small, layers):
    def gathered(weight, width):
        every = lax.all_gather(weight, "fsdp", axis=1, tiled=True)
        every = every.reshape(layers, D, width, D).transpose(0, 2, 1, 3)
        return every.reshape(layers, width, 16, PART, D)

    outward = lax.all_gather(w_out, "fsdp", axis=1, tiled=True)
    outward = outward.reshape(layers, 16, 4, PART, D).transpose(0, 2, 1, 3, 4)
    parts = [gathered(w_qkv, 3), gathered(w_o, 1), gathered(w_in, 4), outward]
    panels = jnp.concatenate(parts, axis=1).transpose(2, 0, 1, 3, 4).reshape(16, -1, D)
    small = lax.psum(small.astype(WIDE), "fsdp").astype(LOW)
    small = jnp.pad(small[None], ((0, 15), (0, 0), (0, 0)))
    return jnp.concatenate([panels, small], axis=1).reshape(4, 2, 2, -1, D)


def far_total(partial, layers, part):
    partial = partial.reshape(16, -1, D).astype(WIDE)
    panels = layers * PANELS
    grads = partial[:, : panels * PART].reshape(16, layers, PANELS, PART, D)
    inner = grads[:, :, :OUT_AT].transpose(1, 2, 0, 3, 4).reshape(layers, OUT_AT, -1, part, D)
    outer = grads[:, :, OUT_AT:].transpose(1, 0, 2, 3, 4).reshape(layers, -1, 4, part, D)
    both = jnp.concatenate([inner.transpose(2, 0, 1, 3, 4), outer.transpose(1, 0, 2, 3, 4)], axis=2)
    total = lax.psum_scatter(both.reshape(-1, panels * part, D), "fsdp", scatter_dimension=0)
    small = lax.psum(partial[0, panels * PART :], ("rep", "fsdp"))
    return jnp.concatenate([lax.psum(total, "rep"), small], axis=0)


def shards(
    hidden,
    qry_len,
    psg_len,
    qry_grad,
    psg_grad,
    w_qkv,
    w_o,
    w_in,
    w_out,
    biases,
    gains,
    in_bias,
    parts,
    near,
):
    layers, part = w_qkv.shape[0], w_qkv.shape[1]
    at = lax.axis_index("fsdp")
    small = small_rows(biases, gains, in_bias, at, parts, part)
    sources = (w_qkv, w_o, w_in, w_out, small)
    if not near:
        sources = (far_whole(*sources, layers),)
    whole, mixed, kept = forward(hidden, qry_len, psg_len, sources, layers, near)
    found = backward(qry_grad, psg_grad, qry_len, psg_len, whole, kept, layers, near)
    total = found[2] if near else far_total(found[0], layers, part)
    if near:
        return (mixed, found[1], *unpack(total, layers, part))
    panels = layers * PANELS * part
    grads = total[:panels].reshape(layers, PANELS, part, D)
    matrices = [
        grads[:, first:last].transpose(0, 2, 1, 3).reshape(layers, part, -1)
        for first, last in ((Q_AT, O_AT), (O_AT, IN_AT), (IN_AT, OUT_AT))
    ]
    matrices.append(grads[:, OUT_AT:].reshape(layers, 4 * part, D))
    small = lax.dynamic_slice(total, (panels, at * part), (HIDDEN_ROW, part))
    span = D // (4 * part)
    d_in_bias = total[panels + HIDDEN_ROW : panels + SMALL_ROWS].reshape(layers, 4, D)
    d_in_bias = lax.dynamic_slice(
        d_in_bias, (0, at // span, at % span * 4 * part), (layers, 1, 4 * part)
    )
    return (
        mixed,
        found[1],
        *matrices,
        small[:GAIN_ROW].reshape(layers, 6, part),
        small[GAIN_ROW:].reshape(layers, 2, part),
        d_in_bias.reshape(layers, 4 * part),
    )


def solution(mesh):
    both, cut = ("rep", "fsdp"), P(None, "fsdp")
    rows, last = P(both), P(None, None, "fsdp")
    parts = mesh.shape["fsdp"]
    near = parts == 16 and mesh.shape["rep"] == 2
    return jax.shard_map(
        functools.partial(shards, parts=parts, near=near),
        mesh=mesh,
        in_specs=(rows, rows, rows, rows, rows, cut, cut, cut, cut, last, last, cut),
        out_specs=(rows, rows, cut, cut, cut, cut, last, last, cut),
        check_vma=False,
    )
```

```python
import functools

import jax
import jax.numpy as jnp
from jax import lax
from jax.experimental import pallas as pl
from jax.experimental.pallas import tpu as pltpu
from jax.sharding import PartitionSpec as P

MESH = pl.DeviceIdType.MESH
LOW, WIDE = jnp.bfloat16, jnp.float32
D = 768
HALF = 64
SHORT = 128
LONG = 512
PAIRS = D // 128
NORM_EPS = 1e-12
MASKED = -1e30
VMEM_BYTES = 60 * 2**20
NN = (((1,), (0,)), ((), ()))
NT = (((1,), (1,)), ((), ()))
TN = (((0,), (0,)), ((), ()))

BLK = 16
PAIR = 2 * BLK
LAG = 2
DEPTH = 4
X, Y, Z, CORE = 0, 1, 2, 3
SIZES = {X: 2, Y: 2, Z: 4}
ROUTES = (
    ((X, Z, Y), 0, 128),
    ((Y, Z, X), 128, 128),
    ((Z, X, Y), 256, 256),
    ((Z, Y, X), 512, 256),
)
MINE, THEIRS, SUMMED, FINAL, LAND, HELD = range(6)

Q_AT, K_AT, V_AT, O_AT, IN_AT, OUT_AT, PANELS = 0, 1, 2, 3, 4, 8, 12
PART = D // 16
LAYER_CHUNKS = PANELS * PART // PAIR
GAIN_ROW, HIDDEN_ROW, SMALL_ROWS = 12, 16, 24


def steps_of(axis):
    return (1, 2, 3) if axis == Z else (1,)


class Place:
    def __init__(self):
        core = lax.axis_index("rep")
        spot = lax.axis_index("fsdp")
        x, y, z = lax.rem(spot, 2), lax.rem(spot // 2, 2), spot // 4
        self.core = core
        self.at = {X: x, Y: y, Z: z}
        self.to = {
            (CORE, 1): (1 - core, spot),
            (X, 1): (core, spot + 1 - 2 * x),
            (Y, 1): (core, spot + 2 - 4 * y),
        }
        self.next_z = {}
        for step in (1, 2, 3):
            other = lax.rem(z + step, 4)
            self.next_z[step] = other
            self.to[Z, step] = (core, other * 4 + y * 2 + x)

    def greet(self):
        barrier = pltpu.get_barrier_semaphore()
        for device in self.to.values():
            pl.semaphore_signal(barrier, inc=1, device_id=device, device_id_type=MESH)
        pl.semaphore_wait(barrier, len(self.to))


STAGES = 5


def when_in(chunk, count, work):
    pl.when(jnp.logical_and(chunk >= 0, chunk < count))(work)


class Rounds:
    stages = 0

    def __init__(self, place, send, recv, local, count):
        self.place, self.send, self.recv, self.local, self.count = place, send, recv, local, count
        self.rounds = count + self.stages * LAG

    def remote(self, source, target, stage, slot, partner):
        return pltpu.make_async_remote_copy(
            src_ref=source,
            dst_ref=target,
            send_sem=self.send.at[stage, slot],
            recv_sem=self.recv.at[stage, slot],
            device_id=self.place.to[partner],
            device_id_type=MESH,
        )

    def await_all(self, chunk, stage):
        slot = lax.rem(chunk, DEPTH)
        as_large = self.as_large(stage)
        for semaphores in (self.send, self.recv):
            pltpu.make_async_copy(as_large, as_large, semaphores.at[stage, slot]).wait()
        for copy in self.local_copies(chunk, stage):
            copy.wait()

    def rows(self, chunk, core):
        return pl.ds(pl.multiple_of(self.spot(chunk) * PAIR + core * BLK, BLK), BLK)

    def finish(self, number):
        for stage in range(self.stages):
            chunk = number - LAG * stage - LAG

            def work(chunk=chunk, stage=stage):
                self.await_all(chunk, stage)
                self.finished(chunk, stage)

            when_in(chunk, self.count, work)

    def begin(self, number):
        for stage in range(self.stages):
            chunk = number - LAG * stage

            def work(chunk=chunk, stage=stage):
                for copy in self.local_copies(chunk, stage) + self.copies(chunk, stage):
                    copy.start()

            when_in(chunk, self.count, work)

    def round(self, number):
        self.finish(number)
        self.begin(number)

    def drain(self, begin):
        def body(step, carry):
            number = begin + 2 * step
            self.finish(number)
            self.finish(number + 1)
            self.begin(number)
            self.begin(number + 1)
            return carry

        lax.fori_loop(0, (self.rounds - begin + 1) // 2, body, 0)

    def tiles(self, stage):
        count = 0
        for order, _first, width in ROUTES:
            blocks = 1
            for axis in order[:stage]:
                blocks *= SIZES[axis]
            count += blocks * (width // 128) * len(steps_of(order[stage]))
        return count

    def local_copies(self, chunk, stage):
        return []

    def finished(self, chunk, stage):
        pass


class Gather(Rounds):
    stages = 4

    def __init__(self, own, whole, *rest):
        super().__init__(*rest)
        self.own, self.whole = own, whole

    def spot(self, chunk):
        return lax.rem(chunk + self.count - 1, self.count)

    def copies(self, chunk, stage):
        at = self.place.at
        slot = lax.rem(chunk, DEPTH)
        rows = self.rows(chunk, self.place.core)
        if stage == 3:
            part = self.whole.at[:, :, :, rows, :]
            return [self.remote(part, part, stage, slot, (CORE, 1))]
        found = []
        for route, (order, first, width) in enumerate(ROUTES):
            axis, done = order[stage], order[:stage]
            columns = pl.ds(first, width)
            if stage == 0:
                source = self.own.at[rows, columns]
                part = self.whole.at[at[Z], at[Y], at[X], rows, columns]
            else:
                spans = [
                    pl.ds(0, SIZES[name]) if name in done else pl.ds(at[name], 1)
                    for name in (Z, Y, X)
                ]
                source = part = self.whole.at[spans[0], spans[1], spans[2], rows, columns]
            for step in steps_of(axis):
                found.append(self.remote(source, part, stage, slot, (axis, step)))
        return found

    def as_large(self, stage):
        if stage == 3:
            return self.whole.at[:, :, :, pl.ds(0, BLK), :]
        return self.whole.at[0, 0, 0, pl.ds(0, BLK * self.tiles(stage)), pl.ds(0, 128)]

    def local_copies(self, chunk, stage):
        if stage:
            return []
        at = self.place.at
        rows = self.rows(chunk, self.place.core)
        return [
            pltpu.make_async_copy(
                self.own.at[rows, :],
                self.whole.at[at[Z], at[Y], at[X], rows, :],
                self.local.at[0, lax.rem(chunk, DEPTH)],
            )
        ]


class Scatter(Rounds):
    stages = 5

    def __init__(self, partial, total, work, *rest):
        super().__init__(*rest)
        self.partial, self.total, self.work = partial, total, work

    def spot(self, chunk):
        return lax.rem(2 * self.count - 2 - chunk, self.count)

    def copies(self, chunk, stage):
        core, at = self.place.core, self.place.at
        slot = lax.rem(chunk, DEPTH)
        rows = self.rows(chunk, core)
        if stage == 0:
            theirs = self.partial.at[:, :, :, self.rows(chunk, 1 - core), :]
            landing = self.work[THEIRS].at[slot]
            return [self.remote(theirs, landing, stage, slot, (CORE, 1))]
        if stage == 4:
            source, target = self.work[FINAL].at[slot], self.total.at[rows, :]
            return [self.remote(source, target, stage, slot, (CORE, 1))]
        found = []
        for route, (gather_order, first, width) in enumerate(ROUTES):
            order = gather_order[::-1]
            axis, left = order[stage - 1], [n for n in (Z, Y, X) if n not in order[: stage - 1]]
            if stage == 1:
                held, columns = self.work[SUMMED].at[slot], pl.ds(first, width)
            else:
                held, columns = self.work[HELD, route, stage - 1].at[slot], slice(None)
            landing = self.work[LAND, route, stage].at[slot]
            for step in steps_of(axis):
                to = self.place.next_z[step] if axis == Z else 1 - at[axis]
                index = tuple(to if name == axis else slice(None) for name in left)
                found.append(
                    self.remote(
                        held.at[index + (slice(None), columns)],
                        landing.at[step - 1] if axis == Z else landing,
                        stage,
                        slot,
                        (axis, step),
                    )
                )
        return found

    def as_large(self, stage):
        if stage == 0:
            return self.work[THEIRS].at[0]
        if stage == 4:
            return self.work[FINAL].at[0]
        return self.partial.at[0, 0, 0, pl.ds(0, BLK * self.tiles(3 - stage)), pl.ds(0, 128)]

    def local_copies(self, chunk, stage):
        slot = lax.rem(chunk, DEPTH)
        rows = self.rows(chunk, self.place.core)
        if stage == 0:
            mine = self.partial.at[:, :, :, rows, :]
            return [pltpu.make_async_copy(mine, self.work[MINE].at[slot], self.local.at[0, slot])]
        if stage == 4:
            final = self.work[FINAL].at[slot]
            return [pltpu.make_async_copy(final, self.total.at[rows, :], self.local.at[1, slot])]
        return []

    def finished(self, chunk, stage):
        at = self.place.at
        slot = lax.rem(chunk, DEPTH)
        if stage == 0:
            self.work[SUMMED][slot] = self.work[MINE][slot] + self.work[THEIRS][slot]
        if stage in (0, 4):
            return
        for route, (gather_order, first, width) in enumerate(ROUTES):
            order = gather_order[::-1]
            axis, left = order[stage - 1], [n for n in (Z, Y, X) if n not in order[: stage - 1]]
            if stage == 1:
                held, columns = self.work[SUMMED], slice(first, first + width)
            else:
                held, columns = self.work[HELD, route, stage - 1], slice(None)
            index = tuple(at[axis] if name == axis else slice(None) for name in left)
            value = held[(slot,) + index + (slice(None), columns)]
            landing = self.work[LAND, route, stage]
            if axis == Z:
                value = value.astype(WIDE)
                for step in (1, 2, 3):
                    value = value + landing[slot, step - 1].astype(WIDE)
            elif stage == 3:
                value = value.astype(WIDE) + landing[slot].astype(WIDE)
            else:
                value = value + landing[slot]
            if stage == 3:
                self.work[FINAL][slot, :, first : first + width] = value
            else:
                self.work[HELD, route, stage][slot] = value.astype(LOW)


def scatter_scratch():
    shapes = {
        MINE: ((4, 2, 2, BLK, D), LOW),
        THEIRS: ((4, 2, 2, BLK, D), LOW),
        SUMMED: ((4, 2, 2, BLK, D), LOW),
        FINAL: ((BLK, D), WIDE),
    }
    for route, (gather_order, first, width) in enumerate(ROUTES):
        order = gather_order[::-1]
        for stage in (1, 2, 3):
            left = tuple(SIZES[n] for n in (Z, Y, X) if n not in order[:stage])
            steps = (3,) if order[stage - 1] == Z else ()
            shapes[LAND, route, stage] = (steps + left + (BLK, width), LOW)
            if stage < 3:
                shapes[HELD, route, stage] = (left + (BLK, width), LOW)
    return shapes


def advance(rounds, begin, end):
    if rounds is None:
        return

    def body(number, carry):
        rounds.round(number)
        return carry

    lax.fori_loop(begin, end, body, 0)


class Pending:
    def __init__(self, semaphores):
        self.semaphores, self.known, self.flying = semaphores, {}, {}

    def start(self, key, source, target):
        self.wait(key)
        at = self.known.setdefault(key, len(self.known))
        copy = pltpu.make_async_copy(source, target, self.semaphores.at[at])
        copy.start()
        self.flying[key] = copy

    def wait(self, *keys):
        for key in keys:
            copy = self.flying.pop(key, None)
            if copy is not None:
                copy.wait()

    def wait_all(self):
        self.wait(*list(self.flying))


def dot(left, right, numbers):
    return lax.dot_general(left, right, numbers, preferred_element_type=WIDE)


def norm_parts(resid):
    average = jnp.mean(resid, axis=-1, keepdims=True)
    centered = resid - average
    spread = jnp.mean(centered * centered, axis=-1, keepdims=True)
    scale = lax.rsqrt(spread + NORM_EPS)
    return centered * scale, scale


def column_sum(value):
    return jnp.sum(value, axis=0, keepdims=True)


def lanes_of(pair):
    return pl.ds(pl.multiple_of(pair * 128, 128), 128)


def sequences(qry_len, psg_len):
    return (
        (2 * SHORT, LONG, psg_len[0]),
        (0, SHORT, qry_len[0]),
        (SHORT, SHORT, qry_len[1]),
    )


def rows_in(size, work):
    def body(step, carry):
        work(pl.ds(pl.multiple_of(step * size, size), size))
        return carry

    lax.fori_loop(0, D // size, body, 0)


def section(ref, layer, first, panels):
    return ref.at[:, :, :, pl.ds((layer * PANELS + first) * PART, panels * PART), :]


def matrix(ref):
    return ref[...].reshape(-1, D)


FORWARD_BLOCK = 512
BACKWARD_BLOCK = 512


def place_lanes(shape):
    lane = lax.broadcasted_iota(jnp.int32, shape, 1)
    return lane // HALF, lane % HALF


def dead_rows(length, live):
    row = lax.broadcasted_iota(jnp.int32, (length, 128), 0)
    return jnp.where(row < live, 0.0, MASKED).astype(LOW)


def three_parts(value):
    high = value.astype(LOW)
    rest = value - high.astype(WIDE)
    middle = rest.astype(LOW)
    return high, middle, (rest - middle.astype(WIDE)).astype(LOW)


def attend(pair, packed, extended, context, spans):
    lanes = lanes_of(pair)
    for first, length, live in spans:
        size = min(length, FORWARD_BLOCK)
        head, lane = place_lanes((length, 128))
        keys = packed[1, first : first + length, lanes]
        values = packed[2, first : first + length, lanes]
        dead = jnp.where(lane == 0, dead_rows(length, live), jnp.zeros((), LOW))
        my_keys = [jnp.where(head == which, keys, dead) for which in range(2)]
        my_values = [jnp.where(head == which, values, jnp.ones((), LOW)) for which in range(2)]
        head, lane = place_lanes((size, 128))
        unit = jnp.where(lane == 0, 1.0, 0.0).astype(LOW)
        for start in range(first, first + length, size):
            queries = packed[0, start : start + size, lanes] * jnp.array(HALF**-0.5, LOW)
            found = []
            for which in range(2):
                mine = jnp.where(head == which, queries, unit)
                scores = dot(mine, my_keys[which], NT)
                highest = jnp.max(scores, axis=-1, keepdims=True)
                raised = jnp.exp(scores - highest).astype(LOW)
                result = dot(raised, my_values[which], NN)
                found.append(result / pltpu.roll(result, HALF, axis=1))
                parts = three_parts(-(highest + jnp.log(result)))
                for at, value in enumerate(parts):
                    unit_at = jnp.logical_and(head != which, lane == at + 1)
                    mine = jnp.where(unit_at, value, mine)
                extended[2 * pair + which, start : start + size, :] = mine
            context[start : start + size, lanes] = jnp.where(
                head == 0, found[0], found[1]
            ).astype(LOW)


def attend_back(pair, packed, extended, context, d_context, d_packed, d_keys, d_values, spans):
    lanes = lanes_of(pair)
    for first, length, live in spans:
        size = min(length, BACKWARD_BLOCK)
        head, lane = place_lanes((length, 128))
        keys = packed[1, first : first + length, lanes]
        values = packed[2, first : first + length, lanes]
        blank = jnp.zeros_like(keys)
        ones = jnp.where(jnp.logical_and(lane >= 1, lane <= 3), 1.0, 0.0).astype(LOW)
        dead = jnp.where(lane == 0, dead_rows(length, live), ones)
        only_keys = [jnp.where(head == which, keys, blank) for which in range(2)]
        my_keys = [jnp.where(head == which, keys, dead) for which in range(2)]
        my_values = [jnp.where(head == which, values, ones) for which in range(2)]
        both_keys = jnp.concatenate(only_keys, axis=0)
        head, lane = place_lanes((size, 128))
        blank = jnp.zeros((size, 128), LOW)
        for start in range(first, first + length, size):
            upstream = d_context[start : start + size, lanes]
            product = upstream.astype(WIDE) * context[start : start + size, lanes].astype(WIDE)
            all_probs, all_scores, all_queries, all_upstream = [], [], [], []
            for which in range(2):
                queries = extended[2 * pair + which, start : start + size, :]
                mine = jnp.where(head == which, upstream, blank)
                all_queries.append(jnp.where(head == which, queries, blank))
                all_upstream.append(mine)
                inner = jnp.sum(jnp.where(head == which, product, 0.0), axis=1, keepdims=True)
                parts = three_parts(jnp.broadcast_to(-inner, (size, 128)))
                for at, value in enumerate(parts):
                    unit_at = jnp.logical_and(head != which, lane == at + 1)
                    mine = jnp.where(unit_at, value, mine)
                probs = jnp.exp(dot(my_keys[which], queries, NT))
                d_scores = probs * dot(my_values[which], mine, NT)
                all_probs.append(probs.astype(LOW))
                all_scores.append(d_scores.astype(LOW))
            d_packed[start : start + size, lanes] = (
                dot(jnp.concatenate(all_scores, axis=0), both_keys, TN) * (HALF**-0.5)
            ).astype(LOW)
            k_now = dot(
                jnp.concatenate(all_scores, axis=1), jnp.concatenate(all_queries, axis=0), NN
            )
            v_now = dot(
                jnp.concatenate(all_probs, axis=1), jnp.concatenate(all_upstream, axis=0), NN
            )
            if size < length:
                if start > first:
                    k_now = d_keys[...] + k_now
                    v_now = d_values[...] + v_now
                if start + size < first + length:
                    d_keys[...] = k_now
                    d_values[...] = v_now
                    continue
            d_packed[first : first + length, lanes_of(PAIRS + pair)] = k_now.astype(LOW)
            d_packed[first : first + length, lanes_of(2 * PAIRS + pair)] = v_now.astype(LOW)


KEPT_LOW, PACKED, CONTEXT, EXTENDED, FIRST_LOW, ACTIVE, SLOPE, FIRST_RESID, SECOND_RESID = range(9)
KEPT = (
    ((D, D), LOW),
    ((3, D, D), LOW),
    ((D, D), LOW),
    ((2 * PAIRS, D, 128), LOW),
    ((D, D), LOW),
    ((4, D, D), LOW),
    ((4, D, D), LOW),
    ((D, D), WIDE),
    ((D, D), WIDE),
)
WEIGHT, READY, SMALL, OWN = 10, 11, 12, 13


def forward_kernel(near, layers, count, *refs):
    hidden, qry_len, psg_len = refs[:3]
    if near:
        w_qkv, w_o, w_in, w_out, small_own, whole = refs[3:9]
        refs = refs[9:]
    else:
        whole, refs = refs[3], refs[4:]
    mixed, kept, refs = refs[0], refs[1 : 1 + len(KEPT)], refs[1 + len(KEPT) :]
    (state, total, resid, low, packed, context, extended, first_low, active, slope) = refs[:10]
    (attention_weights, in_weights, out_weights, small, params, semaphores) = refs[10:16]
    rounds = None
    copies = Pending(semaphores)
    if near:
        place, own = Place(), refs[16]
        for layer in range(layers):
            base = layer * PANELS
            blocks = [(w_qkv, 3, Q_AT), (w_o, 1, O_AT), (w_in, 4, IN_AT)]
            for ref, panels, first in blocks:
                for panel in range(panels):
                    copies.start(
                        (OWN, layer, first + panel),
                        ref.at[layer, :, pl.ds(panel * D, D)],
                        own.at[pl.ds((base + first + panel) * PART, PART), :],
                    )
            copies.start(
                (OWN, layer, OUT_AT),
                w_out.at[layer],
                own.at[pl.ds((base + OUT_AT) * PART, 4 * PART), :],
            )
        copies.start((OWN, layers, 0), small_own, own.at[pl.ds(layers * PANELS * PART, PAIR), :])
        place.greet()
        copies.wait_all()
        rounds = Gather(own, whole, place, *refs[17:20], count)
    spans = sequences(qry_len, psg_len)

    def keep(which, layer, ref, panel=None):
        target = kept[which].at[layer] if panel is None else kept[which].at[layer, panel]
        copies.start((which, panel), ref, target)

    def fetch(panel, layer, target):
        copies.start((WEIGHT, panel), section(whole, layer, panel, 1), target)

    spent = [0]

    def run(end):
        if near:
            end = min(end, rounds.rounds)
        if end > spent[0]:
            advance(rounds, spent[0], end)
            spent[0] = end

    run(9)
    copies.start(SMALL, whole.at[:, :, :, pl.ds(layers * PANELS * PART, PAIR), :], small)
    state[...] = hidden[...].astype(WIDE)
    low[...] = hidden[...]
    keep(KEPT_LOW, 0, low)
    copies.wait(SMALL)
    params[...] = jnp.sum(small[...].astype(WIDE), axis=(0, 1, 2))

    def row(at):
        return params[pl.ds(at, 1), :]

    run(14)
    for panel in (Q_AT, K_AT, V_AT):
        fetch(panel, 0, attention_weights.at[panel])
    for layer in range(layers):
        base = LAYER_CHUNKS * layer
        copies.wait((PACKED, None))
        for panel in (Q_AT, K_AT, V_AT):
            copies.wait((WEIGHT, panel))
            value = dot(low[...], matrix(attention_weights.at[panel]), NN)
            if panel != K_AT:
                value = value + row(6 * layer + (0 if panel == Q_AT else 1))
            packed[panel] = value.astype(LOW)
            run(base + 15 + panel)
        keep(PACKED, layer, packed)
        fetch(O_AT, layer, attention_weights.at[O_AT])
        fetch(IN_AT, layer, in_weights.at[0])
        copies.wait((CONTEXT, None), (EXTENDED, None))

        def heads(pair, carry):
            attend(pair, packed, extended, context, spans)
            advance(rounds, base + 17 + pair // 2, base + 17 + (pair + 1) // 2)
            return carry

        lax.fori_loop(0, PAIRS, heads, 0)
        spent[0] = base + 20
        keep(CONTEXT, layer, context)
        keep(EXTENDED, layer, extended)
        fetch(IN_AT + 1, layer, in_weights.at[1])
        copies.wait((WEIGHT, O_AT), (SECOND_RESID, None))
        total[...] = dot(context[...], matrix(attention_weights.at[O_AT]), NN)
        run(base + 21)
        copies.wait((FIRST_RESID, None), (FIRST_LOW, None))

        def normalise_first(rows):
            value = state[rows, :] + (total[rows, :] + row(6 * layer + 2))
            resid[rows, :] = value
            norm = norm_parts(value)[0] * row(GAIN_ROW + 2 * layer) + row(6 * layer + 3)
            first_low[rows, :] = norm.astype(LOW)
            total[rows, :] = norm + row(6 * layer + 4)

        rows_in(128, normalise_first)
        keep(FIRST_RESID, layer, resid)
        keep(FIRST_LOW, layer, first_low)
        for panel in range(4):
            copies.wait((WEIGHT, IN_AT + panel))
            copies.wait((ACTIVE, panel), (SLOPE, panel), (SLOPE, (panel + 2) % 4))

            def inward(rows):
                upward = dot(first_low[rows, :], matrix(in_weights.at[panel % 2]), NN)
                upward = upward + row(HIDDEN_ROW + 4 * layer + panel)
                share = 0.5 + 0.5 * lax.erf(upward * (0.5**0.5))
                bell = jnp.exp(upward * upward * -0.5) * 0.3989422804014327
                active[panel, rows, :] = (upward * share).astype(LOW)
                slope[panel % 2, rows, :] = (share + upward * bell).astype(LOW)

            rows_in(384, inward)
            keep(ACTIVE, layer, active.at[panel], panel)
            keep(SLOPE, layer, slope.at[panel % 2], panel)
            if panel < 2:
                fetch(IN_AT + panel + 2, layer, in_weights.at[panel])
            run(base + 22 + panel)
        run(base + 27)
        for panel in range(4):
            rows = pl.ds((layer * PANELS + OUT_AT) * PART, 4 * PART)
            copies.start(
                (WEIGHT, OUT_AT + panel), whole.at[panel, :, :, rows, :], out_weights.at[panel]
            )
        for panel in range(4):
            copies.wait((WEIGHT, OUT_AT + panel))
            total[...] += dot(active[panel], matrix(out_weights.at[panel]), NN)
            if layer + 1 < layers and panel % 2:
                run(base + 28 + panel // 2)
        if layer + 1 < layers:
            run(base + 32)
            for panel in (Q_AT, K_AT, V_AT):
                fetch(panel, layer + 1, attention_weights.at[panel])
        copies.wait((KEPT_LOW, None))

        def normalise_second(rows):
            norm = norm_parts(total[rows, :])[0]
            value = norm * row(GAIN_ROW + 2 * layer + 1) + row(6 * layer + 5)
            state[rows, :] = value
            low[rows, :] = value.astype(LOW)

        keep(SECOND_RESID, layer, total)
        rows_in(128, normalise_second)
        if layer == layers - 1:
            mixed[...] = low[...]
        else:
            keep(KEPT_LOW, layer + 1, low)
    copies.wait_all()


def vmem(*shape, dtype=LOW):
    return pltpu.VMEM(shape, dtype)


def places():
    return (
        pl.BlockSpec(memory_space=pltpu.VMEM),
        pl.BlockSpec(memory_space=pltpu.SMEM),
        pl.BlockSpec(memory_space=pl.ANY),
    )


def transfer_scratch():
    return [
        pltpu.SemaphoreType.DMA((STAGES, DEPTH)),
        pltpu.SemaphoreType.DMA((STAGES, DEPTH)),
        pltpu.SemaphoreType.DMA((2, DEPTH)),
    ]


def params_of(identity):
    extra = {}
    if identity is not None:
        extra = dict(collective_id=identity, has_side_effects=True)
    return pltpu.CompilerParams(vmem_limit_bytes=VMEM_BYTES, **extra)


def forward(hidden, qry_len, psg_len, sources, layers, near):
    here, scalars, far = places()
    rows = layers * PANELS * PART + PAIR
    outs = [jax.ShapeDtypeStruct((D, D), LOW)]
    outs += [jax.ShapeDtypeStruct((layers,) + s, t) for s, t in KEPT]
    specs = [here] + [far] * len(KEPT)
    if near:
        outs = [jax.ShapeDtypeStruct((4, 2, 2, rows, D), LOW)] + outs
        specs = [far] + specs
    panel = (4, 2, 2, PART, D)
    scratch = [
        vmem(D, D, dtype=WIDE),
        vmem(D, D, dtype=WIDE),
        vmem(D, D, dtype=WIDE),
        vmem(D, D),
        vmem(3, D, D),
        vmem(D, D),
        vmem(2 * PAIRS, D, 128),
        vmem(D, D),
        vmem(4, D, D),
        vmem(2, D, D),
        vmem(4, *panel),
        vmem(2, *panel),
        vmem(4, 2, 2, 4 * PART, D),
        vmem(4, 2, 2, PAIR, D),
        vmem(PAIR, D, dtype=WIDE),
        pltpu.SemaphoreType.DMA((64,)),
    ]
    if near:
        scratch += [vmem(rows, D)] + transfer_scratch()
    found = pl.pallas_call(
        functools.partial(forward_kernel, near, layers, rows // PAIR),
        out_shape=outs,
        in_specs=[here, scalars, scalars] + [far] * len(sources),
        out_specs=specs,
        scratch_shapes=scratch,
        compiler_params=params_of(0 if near else None),
        name="forward",
    )(hidden, qry_len, psg_len, *sources)
    if near:
        return found[0], found[1], found[2:]
    return sources[0], found[0], found[1:]


def backward_kernel(near, layers, count, names, *refs):
    qry_grad, psg_grad, qry_len, psg_len, whole = refs[:5]
    kept, refs = refs[5 : 5 + len(KEPT)], refs[5 + len(KEPT) :]
    partial, d_hidden, refs = refs[0], refs[1], refs[2:]
    if near:
        sums, refs = refs[0], refs[1:]
    targets, refs = dict(zip(HELD_BACK, refs)), refs[len(HELD_BACK) :]
    (slope, flow, d_low, d_context, d_packed, d_upward, attention_weights, in_weights) = refs[:8]
    (out_weights, ready, small, params, grads, d_keys, d_values, semaphores) = refs[8:16]
    rounds = None
    if near:
        place = Place()
        place.greet()
        work = dict(zip(names, refs[19:]))
        rounds = Scatter(partial, sums, work, place, *refs[16:19], count)
    copies = Pending(semaphores)
    spans = sequences(qry_len, psg_len)
    tail = layers * PANELS * PART

    def load(which, layer):
        copies.start(which, kept[which].at[layer], targets[which])

    def fetch(panel, layer, target):
        copies.start((WEIGHT, panel), section(whole, layer, panel, 1), target)

    def fetch_out(layer, panel):
        rows = pl.ds((layer * PANELS + OUT_AT) * PART, 4 * PART)
        copies.start(
            (WEIGHT, OUT_AT + panel), whole.at[panel, :, :, rows, :], out_weights.at[panel % 2]
        )

    def load_hidden(layer, panel):
        copies.start((SLOPE, panel % 2), kept[SLOPE].at[layer, panel], slope.at[panel % 2])
        fetch_out(layer, panel)
        fetch(IN_AT + panel, layer, in_weights.at[panel % 2])

    turn = [0]

    def deliver(value, target, shape):
        at = turn[0] % 4
        turn[0] += 1
        copies.wait((READY, at))
        ready[at] = value.astype(LOW)
        copies.start((READY, at), ready.at[at].reshape(shape), target)

    def pause(end, newest=0):
        copies.wait(*[(READY, (turn[0] + at) % 4) for at in range(4 - newest)])
        run(end)

    def deliver_panel(value, layer, panel):
        deliver(value, section(partial, layer, panel, 1), (4, 2, 2, PART, D))

    def row(at):
        return params[pl.ds(at, 1), :]

    copies.start(SMALL, whole.at[:, :, :, pl.ds(tail, PAIR), :], small)
    for which in (SECOND_RESID, ACTIVE):
        load(which, layers - 1)
    load_hidden(layers - 1, 3)
    for which in (FIRST_LOW, FIRST_RESID, CONTEXT, EXTENDED, PACKED, KEPT_LOW):
        load(which, layers - 1)
    grads[...] = jnp.zeros_like(grads)
    for at, (first, length, live) in enumerate(spans):
        upstream = psg_grad[...] if at == 0 else qry_grad[at - 1 : at, :]
        alive = lax.broadcasted_iota(jnp.int32, (length, D), 0) < live
        flow[first : first + length, :] = jnp.where(alive, upstream, 0.0) / live.astype(WIDE)
    copies.wait(SMALL)
    params[...] = jnp.sum(small[...].astype(WIDE), axis=(0, 1, 2))

    def norm_back(resid, gain, gain_row, shift_row, sum_row):
        def block(rows):
            norm, scale = norm_parts(resid[rows, :])
            upstream = flow[rows, :]
            grads[pl.ds(gain_row, 1), :] += column_sum(upstream * norm)
            grads[pl.ds(shift_row, 1), :] += column_sum(upstream)
            scaled = upstream * gain
            result = (
                scaled
                - jnp.mean(scaled, axis=-1, keepdims=True)
                - norm * jnp.mean(scaled * norm, axis=-1, keepdims=True)
            ) * scale
            grads[pl.ds(sum_row, 1), :] += column_sum(result)
            flow[rows, :] = result
            d_low[rows, :] = result.astype(LOW)

        rows_in(128, block)

    spent = [0]

    def run(end):
        if end > spent[0]:
            advance(rounds, spent[0], end)
            spent[0] = end

    for layer in range(layers - 1, -1, -1):
        base = LAYER_CHUNKS * (layers - 1 - layer)
        copies.wait(SECOND_RESID)
        norm_back(
            targets[SECOND_RESID],
            row(GAIN_ROW + 2 * layer + 1),
            GAIN_ROW + 2 * layer + 1,
            6 * layer + 5,
            6 * layer + 4,
        )
        if layer:
            load(SECOND_RESID, layer - 1)
        copies.wait(ACTIVE)
        for panel in range(4):
            grad = dot(targets[ACTIVE][panel], d_low[...], TN)
            out_rows = pl.ds((layer * PANELS + OUT_AT) * PART, 4 * PART)
            deliver(grad, partial.at[panel, :, :, out_rows, :], (2, 2, 4 * PART, D))
            if base and panel == 1:
                run(base)
        if layer:
            load(ACTIVE, layer - 1)
        for panel in range(3, -1, -1):
            slot = panel % 2
            if panel:
                load_hidden(layer, panel - 1)
            else:
                for at in range(4):
                    fetch(at, layer, attention_weights.at[:, :, :, :, pl.ds(at * D, D)])
            copies.wait((SLOPE, slot), (WEIGHT, OUT_AT + panel))
            value = dot(d_low[...], matrix(out_weights.at[slot]), NT) * slope[slot].astype(WIDE)
            grads[pl.ds(HIDDEN_ROW + 4 * layer + panel, 1), :] = column_sum(value)
            d_upward[...] = value.astype(LOW)
            pause(base + 2 * (3 - panel) + 1)
            copies.wait(FIRST_LOW, (WEIGHT, IN_AT + panel))
            deliver_panel(dot(targets[FIRST_LOW][...], d_upward[...], TN), layer, IN_AT + panel)
            flow[...] += dot(d_upward[...], matrix(in_weights.at[slot]), NT)
            run(base + 2 * (3 - panel) + 2)
        if layer:
            load_hidden(layer - 1, 3)
            load(FIRST_LOW, layer - 1)
        copies.wait(FIRST_RESID)
        norm_back(
            targets[FIRST_RESID],
            row(GAIN_ROW + 2 * layer),
            GAIN_ROW + 2 * layer,
            6 * layer + 3,
            6 * layer + 2,
        )
        if layer:
            load(FIRST_RESID, layer - 1)
        copies.wait(CONTEXT, (WEIGHT, O_AT))
        deliver_panel(dot(targets[CONTEXT][...], d_low[...], TN), layer, O_AT)
        out = attention_weights[:, :, :, :, O_AT * D :].reshape(D, D)
        d_context[...] = dot(d_low[...], out, NT).astype(LOW)
        pause(base + 9)
        copies.wait(PACKED, EXTENDED)

        def heads(pair, carry):
            attend_back(
                pair,
                targets[PACKED],
                targets[EXTENDED],
                targets[CONTEXT],
                d_context,
                d_packed,
                d_keys,
                d_values,
                spans,
            )
            advance(
                rounds, base + 9 + (2 * pair) // 3, base + 9 + (2 * pair + 2) // 3
            )
            return carry

        lax.fori_loop(0, PAIRS, heads, 0)
        spent[0] = base + 13
        if layer:
            for which in (PACKED, EXTENDED, CONTEXT):
                load(which, layer - 1)
        copies.wait(KEPT_LOW, (WEIGHT, 0), (WEIGHT, 1), (WEIGHT, 2))
        for panel in (V_AT, K_AT, Q_AT):
            d_panel = d_packed[:, panel * D : (panel + 1) * D]
            deliver_panel(dot(targets[KEPT_LOW][...], d_panel, TN), layer, panel)
            if panel != K_AT:
                at = 6 * layer + (0 if panel == Q_AT else 1)
                grads[pl.ds(at, 1), :] = column_sum(d_panel.astype(WIDE))
            if panel != V_AT:
                pause(base + 15 + (K_AT - panel), newest=1)
        inward = attention_weights[:, :, :, :, : O_AT * D].reshape(D, O_AT * D)
        flow[...] += dot(d_packed[...], inward, NT)
        pause(base + 17)
        if layer:
            load(KEPT_LOW, layer - 1)
    d_hidden[...] = flow[...].astype(LOW)
    small[...] = jnp.broadcast_to(grads[...].astype(LOW)[None, None, None], small.shape)
    copies.start(SMALL, small, partial.at[:, :, :, pl.ds(tail, PAIR), :])
    copies.wait_all()
    if near:
        rounds.drain(spent[0])


HELD_BACK = (SECOND_RESID, FIRST_RESID, KEPT_LOW, PACKED, CONTEXT, EXTENDED, FIRST_LOW, ACTIVE)


def backward(qry_grad, psg_grad, qry_len, psg_len, whole, kept, layers, near):
    here, scalars, far = places()
    rows = whole.shape[3]
    outs = [jax.ShapeDtypeStruct(whole.shape, LOW), jax.ShapeDtypeStruct((D, D), LOW)]
    specs = [far, here]
    if near:
        outs.append(jax.ShapeDtypeStruct((rows, D), WIDE))
        specs.append(far)
    panel = (4, 2, 2, PART, D)
    scratch = [pltpu.VMEM(*KEPT[which]) for which in HELD_BACK]
    scratch += [
        vmem(2, D, D),
        vmem(D, D, dtype=WIDE),
        vmem(D, D),
        vmem(D, D),
        vmem(D, 3 * D),
        vmem(D, D),
        vmem(4, 2, 2, PART, 4 * D),
        vmem(2, *panel),
        vmem(2, 2, 2, 4 * PART, D),
        vmem(4, D, D),
        vmem(4, 2, 2, PAIR, D),
        vmem(PAIR, D, dtype=WIDE),
        vmem(PAIR, D, dtype=WIDE),
        vmem(LONG, 128, dtype=WIDE),
        vmem(LONG, 128, dtype=WIDE),
        pltpu.SemaphoreType.DMA((32,)),
    ]
    shapes = {}
    if near:
        shapes = scatter_scratch()
        scratch += transfer_scratch()
        scratch += [vmem(DEPTH, *s, dtype=t) for s, t in shapes.values()]
    return pl.pallas_call(
        functools.partial(backward_kernel, near, layers, rows // PAIR, tuple(shapes)),
        out_shape=outs,
        in_specs=[here, here, scalars, scalars, far] + [far] * len(KEPT),
        out_specs=specs,
        scratch_shapes=scratch,
        compiler_params=params_of(1 if near else None),
        name="backward",
    )(qry_grad, psg_grad, qry_len, psg_len, whole, *kept)


def unpack_kernel(layers, part, total, qkv, o, inward, outward, biases, gains, in_bias, semaphores):
    copies = Pending(semaphores)
    for layer in range(layers):
        base = layer * PANELS
        for ref, panels, first in ((qkv, 3, Q_AT), (o, 1, O_AT), (inward, 4, IN_AT)):
            for panel in range(panels):
                copies.start(
                    (layer, first + panel),
                    total.at[pl.ds((base + first + panel) * part, part), :],
                    ref.at[layer, :, pl.ds(panel * D, D)],
                )
        copies.start(
            (layer, OUT_AT),
            total.at[pl.ds((base + OUT_AT) * part, 4 * part), :],
            outward.at[layer],
        )
    at, span, tail = lax.axis_index("fsdp"), D // (4 * part), layers * PANELS * part
    mine = pltpu.roll(total[tail : tail + HIDDEN_ROW, :], D - at * part, axis=1)[:, :part]
    for layer in range(layers):
        biases[layer] = mine[6 * layer : 6 * layer + 6]
        gains[layer] = mine[GAIN_ROW + 2 * layer : GAIN_ROW + 2 * layer + 2]
        row = total[pl.ds(tail + HIDDEN_ROW + 4 * layer + at // span, 1), :]
        row = jnp.broadcast_to(row, (8, D))
        row = pltpu.roll(row, D - lax.rem(at, span) * (4 * part), axis=1)
        in_bias[layer : layer + 1, :] = row[:1, : 4 * part]
    copies.wait_all()


def unpack(total, layers, part):
    here, _scalars, far = places()
    shapes = [(layers, part, 3 * D), (layers, part, D), (layers, part, 4 * D), (layers, 4 * part, D)]
    shapes += [(layers, 6, part), (layers, 2, part), (layers, 4 * part)]
    return pl.pallas_call(
        functools.partial(unpack_kernel, layers, part),
        out_shape=[jax.ShapeDtypeStruct(shape, WIDE) for shape in shapes],
        in_specs=[here],
        out_specs=[far] * 4 + [here] * 3,
        scratch_shapes=[pltpu.SemaphoreType.DMA((32,))],
        compiler_params=pltpu.CompilerParams(vmem_limit_bytes=VMEM_BYTES),
        name="unpack",
    )(total)


def small_rows(biases, gains, in_bias, at, parts, part):
    rows = [biases.reshape(-1, part), gains.reshape(-1, part)]
    span = D // (4 * part)
    lane = lax.broadcasted_iota(jnp.int32, (1, D), 1)
    small = jnp.concatenate(rows, axis=0)
    small = jnp.where(lane // part == at, jnp.tile(small, (1, parts)), jnp.zeros((), small.dtype))
    placed = jnp.tile(in_bias, (1, span))[:, None, :]
    panel = lax.broadcasted_iota(jnp.int32, (1, 4, 1), 1)
    mine = jnp.logical_and(panel == at // span, (lane // (4 * part) == at % span)[None])
    placed = jnp.where(mine, placed, jnp.zeros((), placed.dtype)).reshape(-1, D)
    small = jnp.concatenate([small, placed], axis=0)
    return jnp.pad(small, ((0, PAIR - small.shape[0]), (0, 0)))


def far_whole(w_qkv, w_o, w_in, w_out, small, layers):
    def gathered(weight, width):
        every = lax.all_gather(weight, "fsdp", axis=1, tiled=True)
        every = every.reshape(layers, D, width, D).transpose(0, 2, 1, 3)
        return every.reshape(layers, width, 16, PART, D)

    outward = lax.all_gather(w_out, "fsdp", axis=1, tiled=True)
    outward = outward.reshape(layers, 16, 4, PART, D).transpose(0, 2, 1, 3, 4)
    parts = [gathered(w_qkv, 3), gathered(w_o, 1), gathered(w_in, 4), outward]
    panels = jnp.concatenate(parts, axis=1).transpose(2, 0, 1, 3, 4).reshape(16, -1, D)
    small = lax.psum(small.astype(WIDE), "fsdp").astype(LOW)
    small = jnp.pad(small[None], ((0, 15), (0, 0), (0, 0)))
    return jnp.concatenate([panels, small], axis=1).reshape(4, 2, 2, -1, D)


def far_total(partial, layers, part):
    partial = partial.reshape(16, -1, D).astype(WIDE)
    panels = layers * PANELS
    grads = partial[:, : panels * PART].reshape(16, layers, PANELS, PART, D)
    inner = grads[:, :, :OUT_AT].transpose(1, 2, 0, 3, 4).reshape(layers, OUT_AT, -1, part, D)
    outer = grads[:, :, OUT_AT:].transpose(1, 0, 2, 3, 4).reshape(layers, -1, 4, part, D)
    both = jnp.concatenate([inner.transpose(2, 0, 1, 3, 4), outer.transpose(1, 0, 2, 3, 4)], axis=2)
    total = lax.psum_scatter(both.reshape(-1, panels * part, D), "fsdp", scatter_dimension=0)
    small = lax.psum(partial[0, panels * PART :], ("rep", "fsdp"))
    return jnp.concatenate([lax.psum(total, "rep"), small], axis=0)


def shards(
    hidden,
    qry_len,
    psg_len,
    qry_grad,
    psg_grad,
    w_qkv,
    w_o,
    w_in,
    w_out,
    biases,
    gains,
    in_bias,
    parts,
    near,
):
    layers, part = w_qkv.shape[0], w_qkv.shape[1]
    at = lax.axis_index("fsdp")
    small = small_rows(biases, gains, in_bias, at, parts, part)
    sources = (w_qkv, w_o, w_in, w_out, small)
    if not near:
        sources = (far_whole(*sources, layers),)
    whole, mixed, kept = forward(hidden, qry_len, psg_len, sources, layers, near)
    found = backward(qry_grad, psg_grad, qry_len, psg_len, whole, kept, layers, near)
    total = found[2] if near else far_total(found[0], layers, part)
    if near:
        return (mixed, found[1], *unpack(total, layers, part))
    panels = layers * PANELS * part
    grads = total[:panels].reshape(layers, PANELS, part, D)
    matrices = [
        grads[:, first:last].transpose(0, 2, 1, 3).reshape(layers, part, -1)
        for first, last in ((Q_AT, O_AT), (O_AT, IN_AT), (IN_AT, OUT_AT))
    ]
    matrices.append(grads[:, OUT_AT:].reshape(layers, 4 * part, D))
    small = lax.dynamic_slice(total, (panels, at * part), (HIDDEN_ROW, part))
    span = D // (4 * part)
    d_in_bias = total[panels + HIDDEN_ROW : panels + SMALL_ROWS].reshape(layers, 4, D)
    d_in_bias = lax.dynamic_slice(
        d_in_bias, (0, at // span, at % span * 4 * part), (layers, 1, 4 * part)
    )
    return (
        mixed,
        found[1],
        *matrices,
        small[:GAIN_ROW].reshape(layers, 6, part),
        small[GAIN_ROW:].reshape(layers, 2, part),
        d_in_bias.reshape(layers, 4 * part),
    )


def solution(mesh):
    both, cut = ("rep", "fsdp"), P(None, "fsdp")
    rows, last = P(both), P(None, None, "fsdp")
    parts = mesh.shape["fsdp"]
    near = parts == 16 and mesh.shape["rep"] == 2
    return jax.shard_map(
        functools.partial(shards, parts=parts, near=near),
        mesh=mesh,
        in_specs=(rows, rows, rows, rows, rows, cut, cut, cut, cut, last, last, cut),
        out_specs=(rows, rows, cut, cut, cut, cut, last, last, cut),
        check_vma=False,
    )
```
